32 devices in a mesh: pair: 8 (over z, core), red: 4 (over y, x).
Axes of the slice: x: 2, y: 2, z: 4, core: 2. Of those that a mesh axis runs over, the one named last changes fastest.
Arguments:
- three_center: bfloat16 [2304, 32, 256], P('pair', 'red'), may hold values from -0.375 to 0.375
- occ_src: int32 [32, 8], P('red'), may hold values from 0 to 7, as said below
- occ_block: int32 [32, 8], P('red'), may hold values from 0 to 15
- occ_blocks: bfloat16 [64, 256], P('red'), may hold values from -0.5 to 0.5
- virt_block: int32 [4, 8, 1], P('red'), may hold values from 0 to 15, as said below
- virt_blocks: bfloat16 [4, 16, 256], P('red', 'pair'), may hold values from -1.5 to 1.5
Outputs:
- chi: float32 [2304, 2304], P('pair', 'red')
The draws below stay inside these ranges and needn't reach their ends.
Inputs may be any that keep to these rules, and one draw needn't show every extreme that they name: `occ_src`: the 8 entries of a row are distinct. `virt_block`: every block listed for tile t of a red group lies from (t) * 2 to (t) * 2 + 1.
All inputs are finite; a program needn't handle non-finite values.
Results may differ from the reference program's by a relative error of at most 0.0041.
Values may be sent and summed in bfloat16 or wider, within the bound.
No kernel may reach another device: no remote copies, remote signals or barrier semaphores. Data moves between devices by JAX's collectives and lax.ppermute only.
A program may use at most 128 MiB of HBM per device.

```python
import jax
import jax.numpy as jnp
from jax import lax

BLK = 16
NAUX = 2304
TPD = 1
NT = 8
NTT = 32
NS = 8
NOB = 16
NVB = 2
N_PAIR = 8
N_RED = 4


def draw_occ_src(key, part):
    keys = jax.random.split(key, NTT)
    orders = jax.vmap(lambda single: jax.random.permutation(single, NT))(keys)
    return orders[:, :NS].astype(jnp.int32)


def draw_virt_block(key, part):
    groups = NTT // NT
    base = jax.random.randint(key, (groups, NT, TPD), 0, NVB)
    base = base.at[:, 0, 0].set(0)
    base = base.at[:, NT - 1, TPD - 1].set(NVB - 1)
    offset = jnp.arange(NT, dtype=jnp.int32) // TPD * NVB
    return (base + offset[None, :, None]).astype(jnp.int32)


def touch_ends(array, stream_key, smallest, top_value):
    index_at = [jax.random.randint(jax.random.fold_in(stream_key, axis), (), 0, length) for axis, length in enumerate(array.shape)]
    widest = array.shape.index(max(array.shape))
    neighbour = index_at[:widest] + [(index_at[widest] + 1) % array.shape[widest]] + index_at[widest + 1:]
    return array.at[tuple(index_at)].set(smallest).at[tuple(neighbour)].set(top_value)


def level_of(stream_key, extent, shards, least, largest):
    def one(axis_at, parts):
        heights = jax.random.uniform(jax.random.fold_in(jax.random.fold_in(stream_key, 6), axis_at), (parts,), jnp.float32, least / len(shards), largest / len(shards))
        return jnp.repeat(jnp.exp(heights), extent[axis_at] // parts).reshape((-1,) + (1,) * (len(extent) - axis_at - 1))

    loudness = one(*shards[0])
    for cut in shards[1:]:
        loudness = loudness * one(*cut)
    return loudness


def gaussian(key, shape, spread, reach, shards=(), kind=jnp.bfloat16):
    drawn = spread * jax.random.normal(key, shape, jnp.float32)
    if shards:
        drawn = drawn * level_of(key, shape, shards, -0.22, 0.18)
    return jnp.clip(drawn, -reach, reach).astype(kind)


def setup_inputs(seed: int = 0) -> dict:
    seeds = jax.random.split(jax.random.key(seed), 7)
    return {
        "three_center": gaussian(seeds[0], (NAUX, NTT, BLK * BLK), 0.0625, 0.375, ((0, 8), (1, 4))),
        "occ_src": draw_occ_src(jax.random.fold_in(seeds[6], 71), 0),
        "occ_block": touch_ends(jax.random.randint(seeds[2], (NTT, NS), 0, NOB), jax.random.fold_in(seeds[2], 1), 0, NOB - 1).astype(jnp.int32),
        "occ_blocks": gaussian(seeds[3], (N_RED * NOB, BLK * BLK), (BLK * NS) ** -0.5, 0.5, ((0, 4),)),
        "virt_block": draw_virt_block(jax.random.fold_in(seeds[6], 71), 0),
        "virt_blocks": gaussian(seeds[5], (N_RED, N_PAIR * NVB, BLK * BLK), (BLK * TPD) ** -0.5, 1.5, ((0, 4), (1, 8))),
    }


def reference(three_center, occ_src, occ_block, occ_blocks, virt_block, virt_blocks):
    groups = jnp.arange(N_RED, dtype=jnp.int32)
    owner = (jnp.arange(NT, dtype=jnp.int32) // TPD) * TPD

    def one_group(total, group):
        tiles = lax.dynamic_slice_in_dim(three_center, group * NT, NT, 1)
        blocks = tiles.astype(jnp.float32).reshape(NAUX, NT, BLK, BLK)
        sources = lax.dynamic_slice_in_dim(occ_src, group * NT, NT, 0)
        chosen = lax.dynamic_slice_in_dim(occ_block, group * NT, NT, 0)
        density = lax.dynamic_slice_in_dim(occ_blocks, group * NOB, NOB, 0).astype(jnp.float32).reshape(NOB, BLK, BLK)
        half = jnp.zeros((NAUX, NT, BLK, BLK), jnp.float32)
        for slot in range(NS):
            half = half + jnp.einsum('tml,ptln->ptmn', density[chosen[:, slot]], blocks[:, sources[:, slot]])
        half = lax.optimization_barrier(half.astype(jnp.bfloat16)).astype(jnp.float32)
        virtual = virt_blocks[group].astype(jnp.float32).reshape(-1, BLK, BLK)
        listed = virt_block[group]
        kernel = jnp.zeros((NAUX, NT, BLK, BLK), jnp.float32)
        for column in range(TPD):
            kernel = kernel + jnp.einsum('ptml,tln->ptmn', half[:, owner + column], virtual[listed[:, column]])
        kernel = kernel.astype(jnp.bfloat16).reshape(NAUX, NT * BLK * BLK)
        flat = tiles.reshape(NAUX, NT * BLK * BLK)
        term = lax.dot_general(flat, kernel, (((1,), (1,)), ((), ())), preferred_element_type=jnp.float32)
        return total + term, None

    chi, unused = lax.scan(one_group, jnp.zeros((NAUX, NAUX), jnp.float32), groups)
    return chi
```

```python
import functools

import jax
import jax.numpy as jnp
from jax import lax
from jax.experimental import pallas as pl
from jax.experimental.pallas import tpu as pltpu
from jax.sharding import PartitionSpec as P

BLK = 16
AREA = BLK * BLK
VMEM_BYTES = 48 * 1024 * 1024
CORES = 2
BF16 = jnp.bfloat16
F32 = jnp.float32


def mixing_of(occ_src, occ_block, occ_blocks, ntiles):
    nblocks = occ_blocks.shape[0]
    block_hot = (occ_block[:, :, None] == jnp.arange(nblocks, dtype=jnp.int32)).astype(BF16)
    picked = jnp.einsum("tsb,bk->tsk", block_hot, occ_blocks, preferred_element_type=F32).astype(BF16)
    source_hot = (occ_src[:, :, None] == jnp.arange(ntiles, dtype=jnp.int32)).astype(BF16)
    mixing = jnp.einsum("tsk,tsa->tka", source_hot, picked, preferred_element_type=F32).astype(BF16)
    return mixing.reshape(ntiles, ntiles, BLK, BLK)


def gather_plan(three_center, occ_src, occ_block, occ_blocks, virt_block, virt_blocks):
    aux_rows, ntiles, area = three_center.shape
    tpd = virt_block.shape[2]
    mixing = mixing_of(occ_src, occ_block, occ_blocks, ntiles)
    blocks = three_center.reshape(aux_rows, ntiles, BLK, BLK)
    half = jnp.einsum("tkml,pkln->ptmn", mixing, blocks, preferred_element_type=F32).astype(BF16)
    all_blocks = lax.all_gather(virt_blocks[0], "pair", axis=0, tiled=True)
    listed = virt_block[0].reshape(ntiles // tpd, tpd, tpd)
    block_hot = (listed[..., None] == jnp.arange(all_blocks.shape[0], dtype=jnp.int32)).astype(BF16)
    picked = jnp.einsum("oijb,bk->oijk", block_hot, all_blocks, preferred_element_type=F32).astype(BF16)
    picked = picked.reshape(ntiles // tpd, tpd, tpd, BLK, BLK)
    grouped = half.reshape(aux_rows, ntiles // tpd, tpd, BLK, BLK)
    kernel = jnp.einsum("pojml,oijln->poimn", grouped, picked, preferred_element_type=F32)
    kernel = kernel.reshape(aux_rows, ntiles, area).astype(BF16)
    piece = lax.all_gather(kernel, "pair", axis=0, tiled=True)
    partial_value = lax.dot_general(
        three_center.reshape(aux_rows, ntiles * area),
        piece.reshape(piece.shape[0], ntiles * area),
        (((1,), (1,)), ((), ())),
        preferred_element_type=F32,
    )
    return lax.psum_scatter(partial_value, "red", scatter_dimension=1, tiled=True)


def iota2(shape, dim):
    return lax.broadcasted_iota(jnp.int32, shape, dim)


def prep_body(virt_ref, wide_ref):
    ntiles = wide_ref.shape[0]
    spread_rows = (iota2((AREA, BLK), 0) % BLK == iota2((AREA, BLK), 1)).astype(BF16)
    spread_cols = (iota2((BLK, AREA), 1) // BLK == iota2((BLK, AREA), 0)).astype(BF16)
    same = iota2((AREA, AREA), 0) // BLK == iota2((AREA, AREA), 1) % BLK
    for t in range(ntiles):
        block = virt_ref[t * BLK:(t + 1) * BLK, :]
        rows = lax.dot_general(spread_rows, block, (((1,), (1,)), ((), ())), preferred_element_type=F32)
        full = jnp.dot(rows.astype(BF16), spread_cols, preferred_element_type=F32)
        wide_ref[t] = jnp.where(same, full, 0.0).astype(BF16)


def kernel_rows(tile_ref, mix_ref, wide_ref, out_ref, mixed, halves):
    ntiles = wide_ref.shape[0]
    rows = iota2((AREA, AREA), 0)
    cols = iota2((AREA, AREA), 1)
    swap = ((rows % BLK == cols // BLK) & (rows // BLK == cols % BLK)).astype(BF16)
    for k in range(ntiles):
        turned = lax.dot_general(
            swap, tile_ref[:, k * AREA:(k + 1) * AREA], (((1,), (1,)), ((), ())), preferred_element_type=F32
        ).astype(BF16)
        for n in range(BLK):
            mixed[n, k * BLK:(k + 1) * BLK, :] = turned[n * BLK:(n + 1) * BLK, :]
    mix = mix_ref[...]
    for n in range(BLK):
        half = jnp.dot(mix, mixed[n], preferred_element_type=F32).astype(BF16)
        for t in range(ntiles):
            halves[t, n * BLK:(n + 1) * BLK, :] = half[t * BLK:(t + 1) * BLK, :]
    for t in range(ntiles):
        out_ref[t * AREA:(t + 1) * AREA, :] = jnp.dot(
            wide_ref[t], halves[t], preferred_element_type=F32
        ).astype(BF16)


def k_body(tile_ref, mix_ref, wide_ref, out_ref, mixed, halves):
    kernel_rows(tile_ref, mix_ref, wide_ref, out_ref, mixed, halves)


def early_body(pick_ref, o_ref, p_ref, e_ref, f_ref, ko_ref, ke_ref, kb_ref, own_ref, s1, s2, s3, s4, terms):
    aux = o_ref.shape[0]
    for at, (upper, lower, right) in enumerate(
        ((o_ref, p_ref, ko_ref), (o_ref, p_ref, ke_ref), (o_ref, p_ref, kb_ref), (e_ref, f_ref, kb_ref))
    ):
        right_value = right[...]
        terms[at, :aux, :] = jnp.dot(upper[...], right_value, preferred_element_type=F32)
        terms[at, aux:, :] = jnp.dot(lower[...], right_value, preferred_element_type=F32)
    own = pick_ref[0]
    own_ref[...] = jnp.where(own >= 0, terms[jnp.maximum(own, 0)], 0.0)
    for at, out in enumerate((s1, s2, s3, s4)):
        out[...] = terms[pick_ref[1 + at]].astype(BF16)


def late_body(pick_ref, c_ref, o_ref, p_ref, e_ref, f_ref, mix_ref, wide_ref, own_ref, s1, s2, s3, s4, kt, mixed, halves):
    aux = o_ref.shape[0]
    kernel_rows(c_ref, mix_ref, wide_ref, kt, mixed, halves)
    right = kt[...]
    place = pick_ref[0]
    for upper, outer, at in ((o_ref, e_ref, 0), (p_ref, f_ref, aux)):
        rows = slice(at, at + aux)
        near = jnp.dot(upper[...], right, preferred_element_type=F32)
        far = jnp.dot(outer[...], right, preferred_element_type=F32).astype(BF16)
        sent = near.astype(BF16)
        own_ref[rows, :] = jnp.where(place == 3, near, 0.0)
        for source, out in enumerate((s1, s2, s3)):
            out[rows, :] = jnp.where(place == source, sent, far)
        s4[rows, :] = far


def call(body, outs, ins, scratch=(), smem=0, flops=0, name=None):
    return pl.pallas_call(
        body,
        out_shape=outs,
        in_specs=[pl.BlockSpec(memory_space=pltpu.SMEM)] * smem
        + [pl.BlockSpec(memory_space=pltpu.VMEM)] * (len(ins) - smem),
        out_specs=jax.tree.map(lambda _: pl.BlockSpec(memory_space=pltpu.VMEM), outs),
        scratch_shapes=list(scratch),
        compiler_params=pltpu.CompilerParams(vmem_limit_bytes=VMEM_BYTES),
        cost_estimate=pl.CostEstimate(
            flops=flops, transcendentals=0, bytes_accessed=sum(x.size * x.dtype.itemsize for x in ins)
        ),
        name=name,
    )(*ins)


def shaped(*shape, dtype=BF16):
    return jax.ShapeDtypeStruct(shape, dtype)


def hub_plan(three_center, occ_src, occ_block, occ_blocks, virt_block, virt_blocks):
    aux, ntiles, area = three_center.shape
    depth = ntiles * area
    pair, red = lax.axis_index("pair"), lax.axis_index("red")
    plane, core = pair // CORES, pair % CORES
    near_end = plane < 2

    def along_z(moves):
        return [(CORES * a + c, CORES * b + c) for a, b in moves for c in range(CORES)]

    core_swap = [(i, i ^ 1) for i in range(8)]
    both = ("pair", "red")

    def everywhere(moves):
        full = list(moves) + [((3 - a, 3 - g), (3 - b, 3 - h)) for (a, g), (b, h) in moves]
        return [((CORES * a + c) * 4 + g, (CORES * b + c) * 4 + h) for (a, g), (b, h) in full for c in range(CORES)]

    own_blocks = virt_blocks[0]
    from_planes = [own_blocks] + [
        lax.ppermute(own_blocks, "pair", along_z([(a, a ^ k) for a in range(4)])) for k in (1, 2, 3)
    ]
    tiles = three_center.reshape(aux, depth)
    *from_planes, tiles = lax.optimization_barrier((*from_planes, tiles))

    outer = lax.ppermute(tiles, "pair", along_z([(0, 1), (1, 0), (2, 3), (3, 2)]))
    inner = lax.ppermute(tiles, "pair", along_z([(1, 2), (2, 1)]))
    partner = lax.ppermute(tiles, "pair", core_swap)
    cuts = [(0, 128), (128, 256), (256, aux)]
    far_move = along_z([(0, 2), (3, 1)])
    far = [lax.ppermute(tiles[a:b], "pair", far_move) for a, b in cuts]

    mine = jnp.stack(from_planes)
    theirs = lax.ppermute(mine, "pair", core_swap)
    every = jnp.stack([mine, theirs])
    held = jnp.arange(virt_blocks.shape[1], dtype=jnp.int32)
    sources = jnp.arange(4, dtype=jnp.int32)
    flips = jnp.arange(CORES, dtype=jnp.int32)
    owner = CORES * (plane ^ sources)[None, :] + (core ^ flips)[:, None]
    block_id = (owner[:, :, None] * virt_blocks.shape[1] + held).reshape(-1)
    listed = virt_block[0, :, 0]
    block_hot = (listed[:, None] == block_id[None, :]).astype(BF16)
    picked = jnp.dot(block_hot, every.reshape(-1, area), preferred_element_type=F32).astype(BF16)
    wide = call(
        prep_body, shaped(ntiles, area, area), [picked.reshape(ntiles * BLK, BLK)], name="widen"
    )
    mixing = mixing_of(occ_src, occ_block, occ_blocks, ntiles)
    mix = mixing.transpose(0, 2, 1, 3).reshape(ntiles * BLK, ntiles * BLK)

    def scratch_for(count):
        return [pltpu.VMEM((BLK, ntiles * BLK, count), BF16), pltpu.VMEM((ntiles, area, count), BF16)]

    def kernel_of(rows, name):
        count = rows.shape[0]
        return call(
            k_body, shaped(depth, count), [rows, mix, wide], scratch_for(count),
            flops=2 * count * depth * 3 * area, name=name,
        )

    k_own = kernel_of(tiles, "k_own")
    k_outer = kernel_of(outer, "k_outer")
    k_inner = kernel_of(inner, "k_inner")
    outer_partner = lax.ppermute(outer, "pair", core_swap)

    place = jnp.where(near_end, red, 3 - red)
    at_hub = (plane == 1) | (plane == 2)
    hub_term = jnp.array([1, 0, 2, -1], jnp.int32)
    end_term = jnp.array([0, 1, -1, -1], jnp.int32)
    term_of = jnp.where(at_hub, hub_term, end_term)
    chosen = [term_of[place]] + [term_of[place ^ d] for d in (1, 2, 3)] + [jnp.int32(-1)]
    picks = jnp.stack([chosen[0]] + [jnp.where(x >= 0, x, 3) for x in chosen[1:]]).astype(jnp.int32)
    flops = 2 * 8 * aux * aux * depth
    own_early, *sent = call(
        early_body,
        [shaped(2 * aux, aux, dtype=F32)] + [shaped(2 * aux, aux)] * 4,
        [picks, tiles, partner, outer, outer_partner, k_own, k_outer, k_inner],
        [pltpu.VMEM((4, 2 * aux, aux), F32)],
        smem=1, flops=flops, name="early",
    )
    arrived = []
    for d, value in zip((1, 2, 3), sent):
        moves = [((1, g), (1, g ^ d)) for g in range(4) if g ^ d != 3]
        moves += [((0, g), (0, g ^ d)) for g in range(4) if g ^ d < 2]
        moves += [((1, 3 ^ d), (0, 2))]
        arrived.append(lax.ppermute(value, both, everywhere(moves)))
    arrived.append(lax.ppermute(sent[3], both, everywhere([((1, 3), (0, 2))])))

    late_place = place[None].astype(jnp.int32)
    late_moves = [
        [((1, 0), (1, 3)), ((1, 1), (0, 3))],
        [((1, 1), (1, 3)), ((1, 2), (0, 3))],
        [((1, 2), (1, 3)), ((1, 0), (0, 3))],
        [((1, 3), (0, 3))],
    ]
    late_terms = []
    for (a, b), rows in zip(cuts, far):
        count = b - a
        own_late, *late_sent = call(
            late_body,
            [shaped(2 * aux, count, dtype=F32)] + [shaped(2 * aux, count)] * 4,
            [late_place, rows, tiles, partner, outer, outer_partner, mix, wide],
            [pltpu.VMEM((depth, count), BF16)] + scratch_for(count),
            smem=1, flops=2 * 4 * aux * count * depth, name=f"late_{a}",
        )
        at_plane = jnp.where(at_hub, own_late, 0.0)
        for moves, value in zip(late_moves, late_sent):
            at_plane = at_plane + lax.ppermute(value, both, everywhere(moves)).astype(F32)
        late_terms.append(at_plane)

    total = own_early
    for value in arrived:
        total = total + value.astype(F32)
    total = total + jnp.concatenate(late_terms, axis=1)
    other = lax.ppermute(total[aux:], "pair", core_swap)
    kept = total[:aux]
    return jnp.where(
        core == 0, jnp.concatenate([kept, other], axis=1), jnp.concatenate([other, kept], axis=1)
    )


def solution(mesh):
    placed = (
        P("pair", "red", None),
        P("red", None),
        P("red", None),
        P("red", None),
        P("red", None, None),
        P("red", "pair", None),
    )
    small = mesh.shape["pair"] == 8 and mesh.shape["red"] == 4
    return jax.shard_map(
        hub_plan if small else gather_plan,
        mesh=mesh, in_specs=placed, out_specs=P("pair", "red"), check_vma=False,
    )
```

```python
import functools

import jax
import jax.numpy as jnp
from jax import lax
from jax.experimental import pallas as pl
from jax.experimental.pallas import tpu as pltpu
from jax.sharding import PartitionSpec as P

BLK = 16
AREA = BLK * BLK
VMEM_BYTES = 24 * 1024 * 1024
CORES = 2
BF16 = jnp.bfloat16
F32 = jnp.float32


def mixing_of(occ_src, occ_block, occ_blocks, ntiles):
    nblocks = occ_blocks.shape[0]
    block_hot = (occ_block[:, :, None] == jnp.arange(nblocks, dtype=jnp.int32)).astype(BF16)
    picked = jnp.einsum("tsb,bk->tsk", block_hot, occ_blocks, preferred_element_type=F32).astype(BF16)
    source_hot = (occ_src[:, :, None] == jnp.arange(ntiles, dtype=jnp.int32)).astype(BF16)
    mixing = jnp.einsum("tsk,tsa->tka", source_hot, picked, preferred_element_type=F32).astype(BF16)
    return mixing.reshape(ntiles, ntiles, BLK, BLK)


def gather_plan(three_center, occ_src, occ_block, occ_blocks, virt_block, virt_blocks):
    aux_rows, ntiles, area = three_center.shape
    tpd = virt_block.shape[2]
    mixing = mixing_of(occ_src, occ_block, occ_blocks, ntiles)
    blocks = three_center.reshape(aux_rows, ntiles, BLK, BLK)
    half = jnp.einsum("tkml,pkln->ptmn", mixing, blocks, preferred_element_type=F32).astype(BF16)
    all_blocks = lax.all_gather(virt_blocks[0], "pair", axis=0, tiled=True)
    listed = virt_block[0].reshape(ntiles // tpd, tpd, tpd)
    block_hot = (listed[..., None] == jnp.arange(all_blocks.shape[0], dtype=jnp.int32)).astype(BF16)
    picked = jnp.einsum("oijb,bk->oijk", block_hot, all_blocks, preferred_element_type=F32).astype(BF16)
    picked = picked.reshape(ntiles // tpd, tpd, tpd, BLK, BLK)
    grouped = half.reshape(aux_rows, ntiles // tpd, tpd, BLK, BLK)
    kernel = jnp.einsum("pojml,oijln->poimn", grouped, picked, preferred_element_type=F32)
    kernel = kernel.reshape(aux_rows, ntiles, area).astype(BF16)
    piece = lax.all_gather(kernel, "pair", axis=0, tiled=True)
    partial_value = lax.dot_general(
        three_center.reshape(aux_rows, ntiles * area),
        piece.reshape(piece.shape[0], ntiles * area),
        (((1,), (1,)), ((), ())),
        preferred_element_type=F32,
    )
    return lax.psum_scatter(partial_value, "red", scatter_dimension=1, tiled=True)


def iota2(shape, dim):
    return lax.broadcasted_iota(jnp.int32, shape, dim)


def prep_body(src_ref, block_ref, listed_ref, blocks_ref, mine_ref, theirs_ref, mix_ref, wide_ref, density, held):
    nblocks = blocks_ref.shape[0]
    ntiles, listed_sources = src_ref.shape
    width = ntiles * BLK
    repeat = (iota2((nblocks * BLK, nblocks), 0) // BLK == iota2((nblocks * BLK, nblocks), 1)).astype(BF16)
    rows = jnp.dot(repeat, blocks_ref[...], preferred_element_type=F32)
    rows = jnp.where(iota2(rows.shape, 0) % BLK == iota2(rows.shape, 1) // BLK, rows, 0.0).astype(BF16)
    spread = (iota2((AREA, width), 0) % BLK == iota2((AREA, width), 1) % BLK).astype(BF16)
    density[...] = jnp.dot(rows, spread, preferred_element_type=F32).reshape(nblocks, BLK, width)
    column = iota2((BLK, width), 1) // BLK
    for t in range(ntiles):
        line = jnp.zeros((BLK, width), F32)
        for s in range(listed_sources):
            line = line + jnp.where(column == src_ref[t, s], density[block_ref[t, s]], 0.0)
        mix_ref[t * BLK:(t + 1) * BLK, :] = line.astype(BF16)

    pair = lax.axis_index("pair")
    plane, core = pair // CORES, pair % CORES
    planes, per_owner, _ = mine_ref.shape
    for k in range(planes):
        held[k * per_owner:(k + 1) * per_owner, :] = mine_ref[k].astype(F32)
        held[(planes + k) * per_owner:(planes + k + 1) * per_owner, :] = theirs_ref[k].astype(F32)
    pick = (iota2((AREA, AREA), 0) % BLK == iota2((AREA, AREA), 1) % BLK).astype(F32)
    place = (iota2((AREA, AREA), 0) // BLK == iota2((AREA, AREA), 1) // BLK).astype(BF16)
    same = iota2((AREA, AREA), 0) // BLK == iota2((AREA, AREA), 1) % BLK
    for t in range(ntiles):
        k, flip = plane ^ (t // CORES), core ^ (t % CORES)
        row = (flip * planes + k) * per_owner + listed_ref[0, t, 0] - t * per_owner
        chosen = (pick * held[pl.ds(row, 1), :]).astype(BF16)
        full = jnp.dot(chosen, place, preferred_element_type=F32)
        wide_ref[t] = jnp.where(same, full, 0.0).astype(BF16)


def kernel_rows(tile_ref, mix_ref, wide_ref, out_ref, mixed, halves):
    ntiles = wide_ref.shape[0]
    rows = iota2((AREA, AREA), 0)
    cols = iota2((AREA, AREA), 1)
    swap = ((rows % BLK == cols // BLK) & (rows // BLK == cols % BLK)).astype(BF16)
    for k in range(ntiles):
        turned = lax.dot_general(
            swap, tile_ref[:, k * AREA:(k + 1) * AREA], (((1,), (1,)), ((), ())), preferred_element_type=F32
        ).astype(BF16)
        for n in range(BLK):
            mixed[n, k * BLK:(k + 1) * BLK, :] = turned[n * BLK:(n + 1) * BLK, :]
    mix = mix_ref[...]
    for n in range(BLK):
        half = jnp.dot(mix, mixed[n], preferred_element_type=F32).astype(BF16)
        for t in range(ntiles):
            halves[t, n * BLK:(n + 1) * BLK, :] = half[t * BLK:(t + 1) * BLK, :]
    for t in range(ntiles):
        out_ref[t * AREA:(t + 1) * AREA, :] = jnp.dot(
            wide_ref[t], halves[t], preferred_element_type=F32
        ).astype(BF16)


def k_body(tile_ref, mix_ref, wide_ref, out_ref, mixed, halves):
    kernel_rows(tile_ref, mix_ref, wide_ref, out_ref, mixed, halves)


def place_of():
    plane, red = lax.axis_index("pair") // CORES, lax.axis_index("red")
    near = plane < 2
    return jnp.where(near, plane, 3 - plane), jnp.where(near, red, 3 - red)


def early_body(o_ref, p_ref, e_ref, f_ref, g_ref, ko_ref, ke_ref, kb_ref, own_ref, s1, s2, s3, s4, terms):
    aux = o_ref.shape[0]
    for at, right, lefts in (
        (0, ko_ref, (o_ref, p_ref)),
        (1, ke_ref, (o_ref, p_ref)),
        (2, kb_ref, (o_ref, p_ref)),
        (3, kb_ref, (e_ref, f_ref, g_ref)),
    ):
        right_value = right[...]
        row = 0
        for left in lefts:
            count = left.shape[0]
            terms[at, row:row + count, :] = jnp.dot(left[...], right_value, preferred_element_type=F32)
            row += count
    plane, red = place_of()

    def term_for(column):
        hub = jnp.where(column < 2, 1 - column, column)
        return jnp.where(plane == 1, hub, jnp.minimum(column, 1))

    mine = (plane == 1) & (red < 3) | (plane == 0) & (red < 2)
    own_ref[...] = jnp.where(mine, terms[term_for(red)], 0.0)
    for d, out in zip((1, 2, 3), (s1, s2, s3)):
        out[...] = terms[term_for(red ^ d)].astype(BF16)
    s4[...] = terms[3].astype(BF16)


def late_body(c_ref, o_ref, p_ref, e_ref, f_ref, g_ref, mix_ref, wide_ref, own_ref, s1, s2, s3, s4, near, kt, mixed, halves):
    aux = o_ref.shape[0]
    kernel_rows(c_ref, mix_ref, wide_ref, kt, mixed, halves)
    right = kt[...]
    plane, place = place_of()
    mine = (plane == 1) & (place == 3)
    half = aux // 2
    near_parts = [(o_ref, 0, aux), (p_ref, aux, aux)]
    far_parts = [(e_ref, 0, aux), (f_ref, aux, half), (g_ref, aux + half, half)]
    for left, row, count in near_parts:
        value = jnp.dot(left[...], right, preferred_element_type=F32)
        own_ref[row:row + count, :] = jnp.where(mine, value, 0.0)
        near[row:row + count, :] = value.astype(BF16)
    for left, row, count in far_parts:
        rows = slice(row, row + count)
        value = jnp.dot(left[...], right, preferred_element_type=F32).astype(BF16)
        for source, out in enumerate((s1, s2, s3)):
            out[rows, :] = jnp.where(place == source, near[rows, :], value)
        s4[rows, :] = value


def call(body, outs, ins, scratch=(), smem=0, flops=0, name=None, vmem=VMEM_BYTES):
    return pl.pallas_call(
        body,
        out_shape=outs,
        in_specs=[pl.BlockSpec(memory_space=pltpu.SMEM)] * smem
        + [pl.BlockSpec(memory_space=pltpu.VMEM)] * (len(ins) - smem),
        out_specs=jax.tree.map(lambda _: pl.BlockSpec(memory_space=pltpu.VMEM), outs),
        scratch_shapes=list(scratch),
        compiler_params=pltpu.CompilerParams(vmem_limit_bytes=vmem),
        cost_estimate=pl.CostEstimate(
            flops=1, transcendentals=0, bytes_accessed=1
        ),
        name=name,
    )(*ins)


def shaped(*shape, dtype=BF16):
    return jax.ShapeDtypeStruct(shape, dtype)


def hub_plan(three_center, occ_src, occ_block, occ_blocks, virt_block, virt_blocks):
    aux, ntiles, area = three_center.shape
    depth = ntiles * area
    core = lax.axis_index("pair") % CORES

    def along_z(moves):
        return [(CORES * a + c, CORES * b + c) for a, b in moves for c in range(CORES)]

    core_swap = [(i, i ^ 1) for i in range(8)]
    both = ("pair", "red")

    def everywhere(moves):
        full = list(moves) + [((3 - a, 3 - g), (3 - b, 3 - h)) for (a, g), (b, h) in moves]
        return [((CORES * a + c) * 4 + g, (CORES * b + c) * 4 + h) for (a, g), (b, h) in full for c in range(CORES)]

    after = lax.optimization_barrier

    def scratch_for(count):
        return [pltpu.VMEM((BLK, ntiles * BLK, count), BF16), pltpu.VMEM((ntiles, area, count), BF16)]

    def kernel_of(rows, mix, wide, name):
        count = rows.shape[0]
        return call(
            k_body, shaped(depth, count), [rows, mix, wide], scratch_for(count),
            flops=2 * count * depth * 3 * area, name=name,
        )

    from_planes = [virt_blocks] + [
        lax.ppermute(virt_blocks, "pair", along_z([(a, a ^ k) for a in range(4)])) for k in (1, 2, 3)
    ]
    tiles = three_center.reshape(aux, depth)
    *from_planes, tiles = after((*from_planes, tiles))
    inner = lax.ppermute(tiles, "pair", along_z([(1, 2), (2, 1)]))
    mine = jnp.concatenate(from_planes)
    theirs = lax.ppermute(mine, "pair", core_swap)
    partner = lax.ppermute(tiles, "pair", core_swap)
    theirs, tiles = after((theirs, tiles))
    outer = lax.ppermute(tiles, "pair", along_z([(0, 1), (1, 0), (2, 3), (3, 2)]))
    mix, wide = call(
        prep_body,
        [shaped(ntiles * BLK, ntiles * BLK), shaped(ntiles, area, area)],
        [occ_src, occ_block, virt_block, occ_blocks, mine, theirs],
        [pltpu.VMEM((occ_blocks.shape[0], BLK, ntiles * BLK), F32), pltpu.VMEM((16, area), F32)],
        smem=3, name="prep",
    )
    partner, wide, tiles = after((partner, wide, tiles))
    far = lax.ppermute(tiles, "pair", along_z([(0, 2), (3, 1)]))
    k_own = kernel_of(tiles, mix, wide, "k_own")
    outer, inner, k_own = after((outer, inner, k_own))

    outer_partner = [lax.ppermute(outer[at:at + aux // 2], "pair", core_swap) for at in (0, aux // 2)]
    k_outer = kernel_of(outer, mix, wide, "k_outer")
    k_inner = kernel_of(inner, mix, wide, "k_inner")
    own_early, *sent = call(
        early_body,
        [shaped(2 * aux, aux, dtype=F32)] + [shaped(2 * aux, aux)] * 4,
        [tiles, partner, outer, *outer_partner, k_own, k_outer, k_inner],
        [pltpu.VMEM((4, 2 * aux, aux), F32)],
        flops=2 * 8 * aux * aux * depth, name="early",
    )
    arrived = []
    for d, value in zip((1, 2, 3), sent):
        moves = [((1, g), (1, g ^ d)) for g in range(4) if g ^ d != 3]
        moves += [((0, g), (0, g ^ d)) for g in range(4) if g ^ d < 2]
        moves += [((1, 3 ^ d), (0, 2))]
        arrived.append(lax.ppermute(value, both, everywhere(moves)))
    arrived.append(lax.ppermute(sent[3], both, everywhere([((1, 3), (0, 2))])))

    far, own_early = after((far, own_early))
    own_late, *late_sent = call(
        late_body,
        [shaped(2 * aux, aux, dtype=F32)] + [shaped(2 * aux, aux)] * 4,
        [far, tiles, partner, outer, *outer_partner, mix, wide],
        [pltpu.VMEM((2 * aux, aux), BF16), pltpu.VMEM((depth, aux), BF16)] + scratch_for(aux),
        flops=2 * 4 * aux * aux * depth, name="late",
    )
    late_moves = [
        [((1, 0), (1, 3)), ((1, 1), (0, 3))],
        [((1, 1), (1, 3)), ((1, 2), (0, 3))],
        [((1, 2), (1, 3)), ((1, 0), (0, 3))],
        [((1, 3), (0, 3))],
    ]
    total = own_early
    for value in arrived:
        total = total + value.astype(F32)
    total, *late_sent = after((total, *late_sent))
    total = total + own_late
    for moves, value in zip(late_moves, late_sent):
        total = total + lax.ppermute(value, both, everywhere(moves)).astype(F32)

    other = lax.ppermute(total[aux:], "pair", core_swap)
    kept = total[:aux]
    return jnp.where(
        core == 0, jnp.concatenate([kept, other], axis=1), jnp.concatenate([other, kept], axis=1)
    )


def solution(mesh):
    placed = (
        P("pair", "red", None),
        P("red", None),
        P("red", None),
        P("red", None),
        P("red", None, None),
        P("red", "pair", None),
    )
    small = mesh.shape["pair"] == 8 and mesh.shape["red"] == 4
    return jax.shard_map(
        hub_plan if small else gather_plan,
        mesh=mesh, in_specs=placed, out_specs=P("pair", "red"), check_vma=False,
    )
```

```python
import functools

import jax
import jax.numpy as jnp
from jax import lax
from jax.experimental import pallas as pl
from jax.experimental.pallas import tpu as pltpu
from jax.sharding import PartitionSpec as P

BLK = 16
AREA = BLK * BLK
VMEM_BYTES = 24 * 1024 * 1024
CORES = 2
BF16 = jnp.bfloat16
F32 = jnp.float32


def mixing_of(occ_src, occ_block, occ_blocks, ntiles):
    nblocks = occ_blocks.shape[0]
    block_hot = (occ_block[:, :, None] == jnp.arange(nblocks, dtype=jnp.int32)).astype(BF16)
    picked = jnp.einsum("tsb,bk->tsk", block_hot, occ_blocks, preferred_element_type=F32).astype(BF16)
    source_hot = (occ_src[:, :, None] == jnp.arange(ntiles, dtype=jnp.int32)).astype(BF16)
    mixing = jnp.einsum("tsk,tsa->tka", source_hot, picked, preferred_element_type=F32).astype(BF16)
    return mixing.reshape(ntiles, ntiles, BLK, BLK)


def gather_plan(three_center, occ_src, occ_block, occ_blocks, virt_block, virt_blocks):
    aux_rows, ntiles, area = three_center.shape
    tpd = virt_block.shape[2]
    mixing = mixing_of(occ_src, occ_block, occ_blocks, ntiles)
    blocks = three_center.reshape(aux_rows, ntiles, BLK, BLK)
    half = jnp.einsum("tkml,pkln->ptmn", mixing, blocks, preferred_element_type=F32).astype(BF16)
    all_blocks = lax.all_gather(virt_blocks[0], "pair", axis=0, tiled=True)
    listed = virt_block[0].reshape(ntiles // tpd, tpd, tpd)
    block_hot = (listed[..., None] == jnp.arange(all_blocks.shape[0], dtype=jnp.int32)).astype(BF16)
    picked = jnp.einsum("oijb,bk->oijk", block_hot, all_blocks, preferred_element_type=F32).astype(BF16)
    picked = picked.reshape(ntiles // tpd, tpd, tpd, BLK, BLK)
    grouped = half.reshape(aux_rows, ntiles // tpd, tpd, BLK, BLK)
    kernel = jnp.einsum("pojml,oijln->poimn", grouped, picked, preferred_element_type=F32)
    kernel = kernel.reshape(aux_rows, ntiles, area).astype(BF16)
    piece = lax.all_gather(kernel, "pair", axis=0, tiled=True)
    partial_value = lax.dot_general(
        three_center.reshape(aux_rows, ntiles * area),
        piece.reshape(piece.shape[0], ntiles * area),
        (((1,), (1,)), ((), ())),
        preferred_element_type=F32,
    )
    return lax.psum_scatter(partial_value, "red", scatter_dimension=1, tiled=True)


def iota2(shape, dim):
    return lax.broadcasted_iota(jnp.int32, shape, dim)


def prep_body(src_ref, block_ref, listed_ref, blocks_ref, mine_ref, theirs_ref, mix_ref, wide_ref, density, held):
    nblocks = blocks_ref.shape[0]
    ntiles, listed_sources = src_ref.shape
    width = ntiles * BLK
    repeat = (iota2((nblocks * BLK, nblocks), 0) // BLK == iota2((nblocks * BLK, nblocks), 1)).astype(BF16)
    rows = jnp.dot(repeat, blocks_ref[...], preferred_element_type=F32)
    rows = jnp.where(iota2(rows.shape, 0) % BLK == iota2(rows.shape, 1) // BLK, rows, 0.0).astype(BF16)
    spread = (iota2((AREA, width), 0) % BLK == iota2((AREA, width), 1) % BLK).astype(BF16)
    density[...] = jnp.dot(rows, spread, preferred_element_type=F32).reshape(nblocks, BLK, width)
    column = iota2((BLK, width), 1) // BLK
    for t in range(ntiles):
        line = jnp.zeros((BLK, width), F32)
        for s in range(listed_sources):
            line = line + jnp.where(column == src_ref[t, s], density[block_ref[t, s]], 0.0)
        mix_ref[t * BLK:(t + 1) * BLK, :] = line.astype(BF16)

    pair = lax.axis_index("pair")
    plane, core = pair // CORES, pair % CORES
    planes, per_owner, _ = mine_ref.shape
    for k in range(planes):
        held[k * per_owner:(k + 1) * per_owner, :] = mine_ref[k].astype(F32)
        held[(planes + k) * per_owner:(planes + k + 1) * per_owner, :] = theirs_ref[k].astype(F32)
    pick = (iota2((AREA, AREA), 0) % BLK == iota2((AREA, AREA), 1) % BLK).astype(F32)
    place = (iota2((AREA, AREA), 0) // BLK == iota2((AREA, AREA), 1) // BLK).astype(BF16)
    same = iota2((AREA, AREA), 0) // BLK == iota2((AREA, AREA), 1) % BLK
    for t in range(ntiles):
        k, flip = plane ^ (t // CORES), core ^ (t % CORES)
        row = (flip * planes + k) * per_owner + listed_ref[0, t, 0] - t * per_owner
        chosen = (pick * held[pl.ds(row, 1), :]).astype(BF16)
        full = jnp.dot(chosen, place, preferred_element_type=F32)
        wide_ref[t] = jnp.where(same, full, 0.0).astype(BF16)


NT_DIMS = (((1,), (1,)), ((), ()))


def half_rows(tiles, mix, mixed, halves):
    ntiles = halves.shape[0]
    rows, cols = iota2((AREA, AREA), 0), iota2((AREA, AREA), 1)
    swap = ((rows % BLK == cols // BLK) & (rows // BLK == cols % BLK)).astype(BF16)
    for k in range(ntiles):
        block = jnp.concatenate([ref[:, k * AREA:(k + 1) * AREA] for ref in tiles], axis=0)
        turned = lax.dot_general(swap, block, NT_DIMS, preferred_element_type=F32).astype(BF16)
        for n in range(BLK):
            mixed[n, k * BLK:(k + 1) * BLK, :] = turned[n * BLK:(n + 1) * BLK, :]
    for n in range(BLK):
        half = jnp.dot(mix, mixed[n], preferred_element_type=F32).astype(BF16)
        for t in range(ntiles):
            halves[t, n * BLK:(n + 1) * BLK, :] = half[t * BLK:(t + 1) * BLK, :]


def k_own_body(tile_ref, mix_ref, wide_ref, out_ref, mixed, halves):
    half_rows((tile_ref,), mix_ref[...], mixed, halves)
    for t in range(wide_ref.shape[0]):
        out_ref[:, t * AREA:(t + 1) * AREA] = lax.dot_general(
            halves[t], wide_ref[t], (((0,), (1,)), ((), ())), preferred_element_type=F32
        ).astype(BF16)


def k_moved_body(inner_ref, outer_ref, mix_ref, wide_ref, out_ref, mixed, halves):
    half_rows((inner_ref, outer_ref), mix_ref[...], mixed, halves)
    for t in range(wide_ref.shape[0]):
        out_ref[t * AREA:(t + 1) * AREA, :] = jnp.dot(
            wide_ref[t], halves[t], preferred_element_type=F32
        ).astype(BF16)


def packed(top, bottom):
    half = top.shape[0] // 2
    return jnp.concatenate([top[:half], top[half:], bottom[:half], bottom[half:]], axis=1)


def dot_rows(left, right):
    return lax.dot_general(left, right, NT_DIMS, preferred_element_type=F32)


def near_body(o_ref, p_ref, k_ref, out_ref):
    right = k_ref[...]
    out_ref[...] = packed(dot_rows(o_ref[...], right), dot_rows(p_ref[...], right))


def place_of():
    plane, red = lax.axis_index("pair") // CORES, lax.axis_index("red")
    near = plane < 2
    return jnp.where(near, plane, 3 - plane), jnp.where(near, red, 3 - red)


def early_body(o_ref, p_ref, e_ref, f_ref, g_ref, kt_ref, near_ref, own_ref, s1, s2, s3, held_ref, terms):
    aux = o_ref.shape[0]
    right = kt_ref[...]
    top = jnp.dot(o_ref[...], right, preferred_element_type=F32)
    bottom = jnp.dot(p_ref[...], right, preferred_element_type=F32)
    terms[0] = near_ref[...]
    terms[1] = packed(top[:, aux:], bottom[:, aux:])
    terms[2] = packed(top[:, :aux], bottom[:, :aux])
    inner = kt_ref[:, :aux]
    lower = jnp.concatenate([f_ref[...], g_ref[...]], axis=0)
    terms[3] = packed(
        jnp.dot(e_ref[...], inner, preferred_element_type=F32), jnp.dot(lower, inner, preferred_element_type=F32)
    )
    plane, place = place_of()
    hub = plane == 1

    def term_for(column):
        return jnp.where(hub, jnp.where(column < 2, 1 - column, column), jnp.minimum(column, 1))

    mine = hub & (place < 3) | (plane == 0) & (place < 2)
    own_ref[...] = jnp.where(mine, terms[term_for(place)], 0.0)
    for d, out in zip((1, 2, 3), (s1, s2, s3)):
        out[...] = terms[term_for(place ^ d)].astype(BF16)
    held_ref[...] = terms[3].astype(BF16)


LATE = ((2, 0, None, 1), (0, 2, None, None), (None, None, 0, 2), (None, None, 2, None))
LATE_TO = {0: (1, 3), 1: (0, 2), 2: (0, 3)}


def by_place(place, values):
    chosen = jnp.int32(values[3] or 0)
    for at in (2, 1, 0):
        chosen = jnp.where(place == at, values[at] or 0, chosen)
    return chosen


def late_body(k_ref, o_ref, p_ref, e_ref, f_ref, g_ref, held_ref, own_ref, s1, s2, s3, s4, terms):
    right = k_ref[...]
    plane, place = place_of()
    lower = jnp.concatenate([f_ref[...], g_ref[...]], axis=0)
    near = packed(dot_rows(o_ref[...], right), dot_rows(p_ref[...], right))
    own_ref[...] = jnp.where((plane == 1) & (place == 3), near, 0.0)
    terms[0] = near.astype(BF16)
    terms[1] = held_ref[...]
    terms[2] = packed(dot_rows(e_ref[...], right), dot_rows(lower, right)).astype(BF16)
    for sent, out in zip(LATE, (s1, s2, s3, s4)):
        out[...] = terms[by_place(place, sent)]


def join_body(kept_ref, other_ref, out_ref):
    first = lax.axis_index("pair") % CORES == 0
    kept, other = kept_ref[...], other_ref[...]
    left, right = jnp.where(first, kept, other), jnp.where(first, other, kept)
    half, width = left.shape[0], left.shape[1] // 2
    out_ref[:half, :] = jnp.concatenate([left[:, :width], right[:, :width]], axis=1)
    out_ref[half:, :] = jnp.concatenate([left[:, width:], right[:, width:]], axis=1)


def call(body, outs, ins, scratch=(), smem=0, name=None):
    return pl.pallas_call(
        body,
        out_shape=outs,
        in_specs=[pl.BlockSpec(memory_space=pltpu.SMEM)] * smem
        + [pl.BlockSpec(memory_space=pltpu.VMEM)] * (len(ins) - smem),
        out_specs=jax.tree.map(lambda _: pl.BlockSpec(memory_space=pltpu.VMEM), outs),
        scratch_shapes=list(scratch),
        compiler_params=pltpu.CompilerParams(vmem_limit_bytes=VMEM_BYTES),
        cost_estimate=pl.CostEstimate(
            flops=1, transcendentals=0, bytes_accessed=1
        ),
        name=name,
    )(*ins)


def shaped(*shape, dtype=BF16):
    return jax.ShapeDtypeStruct(shape, dtype)


def hub_plan(three_center, occ_src, occ_block, occ_blocks, virt_block, virt_blocks):
    aux, ntiles, area = three_center.shape
    depth = ntiles * area

    def along_z(moves):
        return [(CORES * a + c, CORES * b + c) for a, b in moves for c in range(CORES)]

    core_swap = [(i, i ^ 1) for i in range(8)]
    both = ("pair", "red")

    def everywhere(moves):
        full = list(moves) + [((3 - a, 3 - g), (3 - b, 3 - h)) for (a, g), (b, h) in moves]
        return [((CORES * a + c) * 4 + g, (CORES * b + c) * 4 + h) for (a, g), (b, h) in full for c in range(CORES)]

    after = lax.optimization_barrier

    def scratch_for(count):
        return [pltpu.VMEM((BLK, ntiles * BLK, count), BF16), pltpu.VMEM((ntiles, area, count), BF16)]

    from_planes = [virt_blocks] + [
        lax.ppermute(virt_blocks, "pair", along_z([(a, a ^ k) for a in range(4)])) for k in (1, 2, 3)
    ]
    tiles = three_center.reshape(aux, depth)
    *from_planes, tiles = after((*from_planes, tiles))
    inner = lax.ppermute(tiles, "pair", along_z([(1, 2), (2, 1)]))
    mine = jnp.concatenate(from_planes)
    theirs = lax.ppermute(mine, "pair", core_swap)
    partner = lax.ppermute(tiles, "pair", core_swap)
    theirs, tiles = after((theirs, tiles))
    outer = lax.ppermute(tiles, "pair", along_z([(0, 1), (1, 0), (2, 3), (3, 2)]))
    mix, wide = call(
        prep_body,
        [shaped(ntiles * BLK, ntiles * BLK), shaped(ntiles, area, area)],
        [occ_src, occ_block, virt_block, occ_blocks, mine, theirs],
        [pltpu.VMEM((occ_blocks.shape[0], BLK, ntiles * BLK), F32), pltpu.VMEM((16, area), F32)],
        smem=3, name="prep",
    )
    partner, wide, tiles = after((partner, wide, tiles))
    k_own = call(k_own_body, shaped(aux, depth), [tiles, mix, wide], scratch_for(aux), name="k_own")
    far = lax.ppermute(k_own, "pair", along_z([(0, 2), (3, 1)]))
    term = (aux // 2, 4 * aux)
    near = call(near_body, shaped(*term, dtype=F32), [tiles, partner, k_own], name="near")
    outer, inner, near = after((outer, inner, near))

    outer_partner = [lax.ppermute(outer[at:at + aux // 2], "pair", core_swap) for at in (0, aux // 2)]
    k_moved = call(
        k_moved_body, shaped(depth, 2 * aux), [inner, outer, mix, wide], scratch_for(2 * aux), name="k_moved"
    )
    own_early, *sent, held = call(
        early_body,
        [shaped(*term, dtype=F32)] + [shaped(*term)] * 4,
        [tiles, partner, outer, *outer_partner, k_moved, near],
        [pltpu.VMEM((4, *term), F32)],
        name="early",
    )
    arrived = []
    for d, value in reversed(list(zip((1, 2, 3), sent))):
        moves = [((1, g), (1, g ^ d)) for g in range(4) if g ^ d != 3]
        moves += [((0, g), (0, g ^ d)) for g in range(4) if g ^ d < 2]
        moves += [((1, 3 ^ d), (0, 2))]
        arrived.append(lax.ppermute(value, both, everywhere(moves)))

    far, held = after((far, held))
    own_late, *late_sent = call(
        late_body,
        [shaped(*term, dtype=F32)] + [shaped(*term)] * 4,
        [far, tiles, partner, outer, *outer_partner, held],
        [pltpu.VMEM((3, *term), BF16)],
        name="late",
    )
    for sources, value in zip(LATE, late_sent):
        moves = [((1, g), LATE_TO[what]) for g, what in enumerate(sources) if what is not None]
        arrived.append(lax.ppermute(value, both, everywhere(moves)))
    total = own_early + own_late
    for value in arrived:
        total = total + value.astype(F32)
    other = lax.ppermute(total[:, 2 * aux:], "pair", core_swap)
    return call(join_body, shaped(aux, 2 * aux, dtype=F32), [total[:, :2 * aux], other], name="join")


def solution(mesh):
    placed = (
        P("pair", "red", None),
        P("red", None),
        P("red", None),
        P("red", None),
        P("red", None, None),
        P("red", "pair", None),
    )
    small = mesh.shape["pair"] == 8 and mesh.shape["red"] == 4
    return jax.shard_map(
        hub_plan if small else gather_plan,
        mesh=mesh, in_specs=placed, out_specs=P("pair", "red"), check_vma=False,
    )
```

```python
import functools

import jax
import jax.numpy as jnp
from jax import lax
from jax.experimental import pallas as pl
from jax.experimental.pallas import tpu as pltpu
from jax.sharding import PartitionSpec as P

BLK = 16
AREA = BLK * BLK
VMEM_BYTES = 24 * 1024 * 1024
CORES = 2
BF16 = jnp.bfloat16
F32 = jnp.float32


def mixing_of(occ_src, occ_block, occ_blocks, ntiles):
    nblocks = occ_blocks.shape[0]
    block_hot = (occ_block[:, :, None] == jnp.arange(nblocks, dtype=jnp.int32)).astype(BF16)
    picked = jnp.einsum("tsb,bk->tsk", block_hot, occ_blocks, preferred_element_type=F32).astype(BF16)
    source_hot = (occ_src[:, :, None] == jnp.arange(ntiles, dtype=jnp.int32)).astype(BF16)
    mixing = jnp.einsum("tsk,tsa->tka", source_hot, picked, preferred_element_type=F32).astype(BF16)
    return mixing.reshape(ntiles, ntiles, BLK, BLK)


def gather_plan(three_center, occ_src, occ_block, occ_blocks, virt_block, virt_blocks):
    aux_rows, ntiles, area = three_center.shape
    tpd = virt_block.shape[2]
    mixing = mixing_of(occ_src, occ_block, occ_blocks, ntiles)
    blocks = three_center.reshape(aux_rows, ntiles, BLK, BLK)
    half = jnp.einsum("tkml,pkln->ptmn", mixing, blocks, preferred_element_type=F32).astype(BF16)
    all_blocks = lax.all_gather(virt_blocks[0], "pair", axis=0, tiled=True)
    listed = virt_block[0].reshape(ntiles // tpd, tpd, tpd)
    block_hot = (listed[..., None] == jnp.arange(all_blocks.shape[0], dtype=jnp.int32)).astype(BF16)
    picked = jnp.einsum("oijb,bk->oijk", block_hot, all_blocks, preferred_element_type=F32).astype(BF16)
    picked = picked.reshape(ntiles // tpd, tpd, tpd, BLK, BLK)
    grouped = half.reshape(aux_rows, ntiles // tpd, tpd, BLK, BLK)
    kernel = jnp.einsum("pojml,oijln->poimn", grouped, picked, preferred_element_type=F32)
    kernel = kernel.reshape(aux_rows, ntiles, area).astype(BF16)
    piece = lax.all_gather(kernel, "pair", axis=0, tiled=True)
    partial_value = lax.dot_general(
        three_center.reshape(aux_rows, ntiles * area),
        piece.reshape(piece.shape[0], ntiles * area),
        (((1,), (1,)), ((), ())),
        preferred_element_type=F32,
    )
    return lax.psum_scatter(partial_value, "red", scatter_dimension=1, tiled=True)


def iota2(shape, dim):
    return lax.broadcasted_iota(jnp.int32, shape, dim)


def prep_body(src_ref, block_ref, listed_ref, blocks_ref, mine_ref, theirs_ref, mix_ref, wide_ref, density, held):
    nblocks = blocks_ref.shape[0]
    ntiles, listed_sources = src_ref.shape
    width = ntiles * BLK
    repeat = (iota2((nblocks * BLK, nblocks), 0) // BLK == iota2((nblocks * BLK, nblocks), 1)).astype(BF16)
    rows = jnp.dot(repeat, blocks_ref[...], preferred_element_type=F32)
    rows = jnp.where(iota2(rows.shape, 0) % BLK == iota2(rows.shape, 1) // BLK, rows, 0.0).astype(BF16)
    spread = (iota2((AREA, width), 0) % BLK == iota2((AREA, width), 1) % BLK).astype(BF16)
    density[...] = jnp.dot(rows, spread, preferred_element_type=F32).reshape(nblocks, BLK, width)
    column = iota2((BLK, width), 1) // BLK
    for t in range(ntiles):
        line = jnp.zeros((BLK, width), F32)
        for s in range(listed_sources):
            line = line + jnp.where(column == src_ref[t, s], density[block_ref[t, s]], 0.0)
        mix_ref[t * BLK:(t + 1) * BLK, :] = line.astype(BF16)

    pair = lax.axis_index("pair")
    plane, core = pair // CORES, pair % CORES
    planes, per_owner, _ = mine_ref.shape
    for k in range(planes):
        held[k * per_owner:(k + 1) * per_owner, :] = mine_ref[k].astype(F32)
        held[(planes + k) * per_owner:(planes + k + 1) * per_owner, :] = theirs_ref[k].astype(F32)
    pick = (iota2((AREA, AREA), 0) % BLK == iota2((AREA, AREA), 1) % BLK).astype(F32)
    place = (iota2((AREA, AREA), 0) // BLK == iota2((AREA, AREA), 1) // BLK).astype(BF16)
    same = iota2((AREA, AREA), 0) // BLK == iota2((AREA, AREA), 1) % BLK
    for t in range(ntiles):
        k, flip = plane ^ (t // CORES), core ^ (t % CORES)
        row = (flip * planes + k) * per_owner + jnp.clip(listed_ref[0, t, 0] - t * per_owner, 0, per_owner - 1)
        chosen = (pick * held[pl.ds(row, 1), :]).astype(BF16)
        full = jnp.dot(chosen, place, preferred_element_type=F32)
        wide_ref[t] = jnp.where(same, full, 0.0).astype(BF16)


NT_DIMS = (((1,), (1,)), ((), ()))


def half_rows(tiles, mix, mixed, halves):
    ntiles = halves.shape[0]
    rows, cols = iota2((AREA, AREA), 0), iota2((AREA, AREA), 1)
    swap = ((rows % BLK == cols // BLK) & (rows // BLK == cols % BLK)).astype(BF16)
    for k in range(ntiles):
        block = jnp.concatenate([ref[:, k * AREA:(k + 1) * AREA] for ref in tiles], axis=0)
        turned = lax.dot_general(swap, block, NT_DIMS, preferred_element_type=F32).astype(BF16)
        for n in range(BLK):
            mixed[n, k * BLK:(k + 1) * BLK, :] = turned[n * BLK:(n + 1) * BLK, :]
    for n in range(BLK):
        half = jnp.dot(mix, mixed[n], preferred_element_type=F32).astype(BF16)
        for t in range(ntiles):
            halves[t, n * BLK:(n + 1) * BLK, :] = half[t * BLK:(t + 1) * BLK, :]


def k_own_body(tile_ref, mix_ref, wide_ref, out_ref, mixed, halves):
    half_rows((tile_ref,), mix_ref[...], mixed, halves)
    for t in range(wide_ref.shape[0]):
        out_ref[:, t * AREA:(t + 1) * AREA] = lax.dot_general(
            halves[t], wide_ref[t], (((0,), (1,)), ((), ())), preferred_element_type=F32
        ).astype(BF16)


def k_moved_body(inner_ref, outer_ref, mix_ref, wide_ref, out_ref, mixed, halves):
    half_rows((inner_ref, outer_ref), mix_ref[...], mixed, halves)
    for t in range(wide_ref.shape[0]):
        out_ref[t * AREA:(t + 1) * AREA, :] = jnp.dot(
            wide_ref[t], halves[t], preferred_element_type=F32
        ).astype(BF16)


def packed(top, bottom):
    half = top.shape[0] // 2
    return jnp.concatenate([top[:half], top[half:], bottom[:half], bottom[half:]], axis=1)


def arranged(top, bottom):
    cut = far_cut(top.shape[1])
    return jnp.concatenate([packed(top[:, :cut], bottom[:, :cut]), packed(top[:, cut:], bottom[:, cut:])], axis=1)


def far_cut(aux):
    return aux // 256 * 256 or aux // 2


def dot_rows(left, right):
    return lax.dot_general(left, right, NT_DIMS, preferred_element_type=F32)


def near_body(o_ref, p_ref, k_ref, out_ref):
    right = k_ref[...]
    out_ref[...] = arranged(dot_rows(o_ref[...], right), dot_rows(p_ref[...], right))


def place_of():
    plane, red = lax.axis_index("pair") // CORES, lax.axis_index("red")
    near = plane < 2
    return jnp.where(near, plane, 3 - plane), jnp.where(near, red, 3 - red)


def early_body(o_ref, p_ref, e_ref, f_ref, g_ref, kt_ref, near_ref, own_ref, s1, s2, s3, held_ref, terms):
    aux = o_ref.shape[0]
    right = kt_ref[...]
    top = jnp.dot(o_ref[...], right, preferred_element_type=F32)
    bottom = jnp.dot(p_ref[...], right, preferred_element_type=F32)
    terms[0] = near_ref[...]
    terms[1] = arranged(top[:, aux:], bottom[:, aux:])
    terms[2] = arranged(top[:, :aux], bottom[:, :aux])
    inner = kt_ref[:, :aux]
    lower = jnp.concatenate([f_ref[...], g_ref[...]], axis=0)
    terms[3] = arranged(
        jnp.dot(e_ref[...], inner, preferred_element_type=F32), jnp.dot(lower, inner, preferred_element_type=F32)
    )
    plane, place = place_of()
    hub = plane == 1

    def term_for(column):
        return jnp.where(hub, jnp.where(column < 2, 1 - column, column), jnp.minimum(column, 1))

    mine = hub & (place < 3) | (plane == 0) & (place < 2)
    own_ref[...] = jnp.where(mine, terms[term_for(place)], 0.0)
    for d, out in zip((1, 2, 3), (s1, s2, s3)):
        out[...] = terms[term_for(place ^ d)].astype(BF16)
    held_ref[...] = terms[3].astype(BF16)


LATE = ((2, 0, None, 1), (0, 2, None, None), (None, None, 0, 2), (None, None, 2, None))
LATE_TO = {0: (1, 3), 1: (0, 2), 2: (0, 3)}


def by_place(place, values):
    chosen = jnp.int32(values[3] or 0)
    for at in (2, 1, 0):
        chosen = jnp.where(place == at, values[at] or 0, chosen)
    return chosen


def late_body(k_ref, o_ref, p_ref, e_ref, f_ref, g_ref, held_ref, own_ref, s1, s2, s3, s4, terms):
    right = k_ref[...]
    plane, place = place_of()
    lower = jnp.concatenate([f_ref[...], g_ref[...]], axis=0)
    near = packed(dot_rows(o_ref[...], right), dot_rows(p_ref[...], right))
    own_ref[...] = jnp.where((plane == 1) & (place == 3), near, 0.0)
    terms[0] = near.astype(BF16)
    terms[1] = held_ref[...]
    terms[2] = packed(dot_rows(e_ref[...], right), dot_rows(lower, right)).astype(BF16)
    for sent, out in zip(LATE, (s1, s2, s3, s4)):
        out[...] = terms[by_place(place, sent)]


def last_body(k_ref, o_ref, p_ref, e_ref, f_ref, g_ref, held_ref, *refs):
    first, (own_ref, s1, s2, s3, s4, terms, own_part, t1, t2, t3, t4) = refs[:5], refs[5:]
    parts = (own_part, t1, t2, t3, t4)
    late_body(k_ref, o_ref, p_ref, e_ref, f_ref, g_ref, held_ref, *parts, terms)
    cut = first[0].shape[1]
    for out, before, part in zip((own_ref, s1, s2, s3, s4), first, parts):
        out[:, :cut] = before[...]
        out[:, cut:] = part[...]


def join_body(kept_ref, other_ref, out_ref):
    first = lax.axis_index("pair") % CORES == 0
    kept, other = kept_ref[...], other_ref[...]
    left, right = jnp.where(first, kept, other), jnp.where(first, other, kept)
    half, aux = left.shape[0], left.shape[1] // 2
    cut = far_cut(aux)
    for at in range(2):
        pieces = [
            piece
            for side in (left, right)
            for piece in (side[:, at * cut:(at + 1) * cut], side[:, 2 * cut + at * (aux - cut):2 * cut + (at + 1) * (aux - cut)])
        ]
        out_ref[at * half:(at + 1) * half, :] = jnp.concatenate(pieces, axis=1)


def call(body, outs, ins, scratch=(), smem=0, name=None):
    return pl.pallas_call(
        body,
        out_shape=outs,
        in_specs=[pl.BlockSpec(memory_space=pltpu.SMEM)] * smem
        + [pl.BlockSpec(memory_space=pltpu.VMEM)] * (len(ins) - smem),
        out_specs=jax.tree.map(lambda _: pl.BlockSpec(memory_space=pltpu.VMEM), outs),
        scratch_shapes=list(scratch),
        compiler_params=pltpu.CompilerParams(vmem_limit_bytes=VMEM_BYTES),
        cost_estimate=pl.CostEstimate(
            flops=1, transcendentals=0, bytes_accessed=1
        ),
        name=name,
    )(*ins)


def shaped(*shape, dtype=BF16):
    return jax.ShapeDtypeStruct(shape, dtype)


def hub_plan(three_center, occ_src, occ_block, occ_blocks, virt_block, virt_blocks):
    aux, ntiles, area = three_center.shape
    depth = ntiles * area

    def along_z(moves):
        return [(CORES * a + c, CORES * b + c) for a, b in moves for c in range(CORES)]

    core_swap = [(i, i ^ 1) for i in range(8)]
    both = ("pair", "red")

    def everywhere(moves):
        full = list(moves) + [((3 - a, 3 - g), (3 - b, 3 - h)) for (a, g), (b, h) in moves]
        return [((CORES * a + c) * 4 + g, (CORES * b + c) * 4 + h) for (a, g), (b, h) in full for c in range(CORES)]

    after = lax.optimization_barrier

    def scratch_for(count):
        return [pltpu.VMEM((BLK, ntiles * BLK, count), BF16), pltpu.VMEM((ntiles, area, count), BF16)]

    from_planes = [virt_blocks] + [
        lax.ppermute(virt_blocks, "pair", along_z([(a, a ^ k) for a in range(4)])) for k in (1, 2, 3)
    ]
    tiles = three_center.reshape(aux, depth)
    *from_planes, tiles = after((*from_planes, tiles))
    inner = lax.ppermute(tiles, "pair", along_z([(1, 2), (2, 1)]))
    mine = jnp.concatenate(from_planes)
    theirs = lax.ppermute(mine, "pair", core_swap)
    partner = lax.ppermute(tiles, "pair", core_swap)
    theirs, tiles = after((theirs, tiles))
    outer = lax.ppermute(tiles, "pair", along_z([(0, 1), (1, 0), (2, 3), (3, 2)]))
    mix, wide = call(
        prep_body,
        [shaped(ntiles * BLK, ntiles * BLK), shaped(ntiles, area, area)],
        [occ_src, occ_block, virt_block, occ_blocks, mine, theirs],
        [pltpu.VMEM((occ_blocks.shape[0], BLK, ntiles * BLK), F32), pltpu.VMEM((16, area), F32)],
        smem=3, name="prep",
    )
    partner, wide, tiles = after((partner, wide, tiles))
    k_own = call(k_own_body, shaped(aux, depth), [tiles, mix, wide], scratch_for(aux), name="k_own")
    cut = far_cut(aux)
    far = [lax.ppermute(part, "pair", along_z([(0, 2), (3, 1)])) for part in (k_own[:cut], k_own[cut:])]
    term = (aux // 2, 4 * aux)
    near = call(near_body, shaped(*term, dtype=F32), [tiles, partner, k_own], name="near")
    outer, inner, near = after((outer, inner, near))

    outer_partner = [lax.ppermute(outer[at:at + aux // 2], "pair", core_swap) for at in (0, aux // 2)]
    k_moved = call(
        k_moved_body, shaped(depth, 2 * aux), [inner, outer, mix, wide], scratch_for(2 * aux), name="k_moved"
    )
    own_early, *sent, held = call(
        early_body,
        [shaped(*term, dtype=F32)] + [shaped(*term)] * 4,
        [tiles, partner, outer, *outer_partner, k_moved, near],
        [pltpu.VMEM((4, *term), F32)],
        name="early",
    )
    arrived = []
    for d, value in reversed(list(zip((1, 2, 3), sent))):
        moves = [((1, g), (1, g ^ d)) for g in range(4) if g ^ d != 3]
        moves += [((0, g), (0, g ^ d)) for g in range(4) if g ^ d < 2]
        moves += [((1, 3 ^ d), (0, 2))]
        arrived.append(lax.ppermute(value, both, everywhere(moves)))

    far[0], held = after((far[0], held))
    part = (aux // 2, 4 * cut)
    first_part = call(
        late_body,
        [shaped(*part, dtype=F32)] + [shaped(*part)] * 4,
        [far[0], tiles, partner, outer, *outer_partner, held[:, :4 * cut]],
        [pltpu.VMEM((3, *part), BF16)],
        name="late",
    )
    far[1], *first_part = after((far[1], *first_part))
    rest = (aux // 2, 4 * (aux - cut))
    own_late, *late_sent = call(
        last_body,
        [shaped(*term, dtype=F32)] + [shaped(*term)] * 4,
        [far[1], tiles, partner, outer, *outer_partner, held[:, 4 * cut:], *first_part],
        [pltpu.VMEM((3, *rest), BF16), pltpu.VMEM(rest, F32)] + [pltpu.VMEM(rest, BF16)] * 4,
        name="last",
    )
    for sources, value in zip(LATE, late_sent):
        moves = [((1, g), LATE_TO[what]) for g, what in enumerate(sources) if what is not None]
        arrived.append(lax.ppermute(value, both, everywhere(moves)))
    total = own_early + own_late
    for value in arrived:
        total = total + value.astype(F32)
    mine, yours = (
        jnp.concatenate([total[:, at * 2 * cut:(at + 1) * 2 * cut], total[:, 4 * cut + at * 2 * (aux - cut):4 * cut + (at + 1) * 2 * (aux - cut)]], axis=1)
        for at in range(2)
    )
    other = lax.ppermute(yours, "pair", core_swap)
    return call(join_body, shaped(aux, 2 * aux, dtype=F32), [mine, other], name="join")


def solution(mesh):
    placed = (
        P("pair", "red", None),
        P("red", None),
        P("red", None),
        P("red", None),
        P("red", None, None),
        P("red", "pair", None),
    )
    small = mesh.shape["pair"] == 8 and mesh.shape["red"] == 4
    return jax.shard_map(
        hub_plan if small else gather_plan,
        mesh=mesh, in_specs=placed, out_specs=P("pair", "red"), check_vma=False,
    )
```

```python
import functools

import jax
import jax.numpy as jnp
from jax import lax
from jax.experimental import pallas as pl
from jax.experimental.pallas import tpu as pltpu
from jax.sharding import PartitionSpec as P

BLK = 16
AREA = BLK * BLK
VMEM_BYTES = 24 * 1024 * 1024
CORES = 2
BF16 = jnp.bfloat16
F32 = jnp.float32


def mixing_of(occ_src, occ_block, occ_blocks, ntiles):
    nblocks = occ_blocks.shape[0]
    block_hot = (occ_block[:, :, None] == jnp.arange(nblocks, dtype=jnp.int32)).astype(BF16)
    picked = jnp.einsum("tsb,bk->tsk", block_hot, occ_blocks, preferred_element_type=F32).astype(BF16)
    source_hot = (occ_src[:, :, None] == jnp.arange(ntiles, dtype=jnp.int32)).astype(BF16)
    mixing = jnp.einsum("tsk,tsa->tka", source_hot, picked, preferred_element_type=F32).astype(BF16)
    return mixing.reshape(ntiles, ntiles, BLK, BLK)


def gather_plan(three_center, occ_src, occ_block, occ_blocks, virt_block, virt_blocks):
    aux_rows, ntiles, area = three_center.shape
    tpd = virt_block.shape[2]
    mixing = mixing_of(occ_src, occ_block, occ_blocks, ntiles)
    blocks = three_center.reshape(aux_rows, ntiles, BLK, BLK)
    half = jnp.einsum("tkml,pkln->ptmn", mixing, blocks, preferred_element_type=F32).astype(BF16)
    all_blocks = lax.all_gather(virt_blocks[0], "pair", axis=0, tiled=True)
    listed = virt_block[0].reshape(ntiles // tpd, tpd, tpd)
    block_hot = (listed[..., None] == jnp.arange(all_blocks.shape[0], dtype=jnp.int32)).astype(BF16)
    picked = jnp.einsum("oijb,bk->oijk", block_hot, all_blocks, preferred_element_type=F32).astype(BF16)
    picked = picked.reshape(ntiles // tpd, tpd, tpd, BLK, BLK)
    grouped = half.reshape(aux_rows, ntiles // tpd, tpd, BLK, BLK)
    kernel = jnp.einsum("pojml,oijln->poimn", grouped, picked, preferred_element_type=F32)
    kernel = kernel.reshape(aux_rows, ntiles, area).astype(BF16)
    piece = lax.all_gather(kernel, "pair", axis=0, tiled=True)
    partial_value = lax.dot_general(
        three_center.reshape(aux_rows, ntiles * area),
        piece.reshape(piece.shape[0], ntiles * area),
        (((1,), (1,)), ((), ())),
        preferred_element_type=F32,
    )
    return lax.psum_scatter(partial_value, "red", scatter_dimension=1, tiled=True)


def iota2(shape, dim):
    return lax.broadcasted_iota(jnp.int32, shape, dim)


def prep_body(src_ref, block_ref, listed_ref, blocks_ref, mine_ref, theirs_ref, mix_ref, wide_ref, density, held):
    nblocks = blocks_ref.shape[0]
    ntiles, listed_sources = src_ref.shape
    width = ntiles * BLK
    repeat = (iota2((nblocks * BLK, nblocks), 0) // BLK == iota2((nblocks * BLK, nblocks), 1)).astype(BF16)
    rows = jnp.dot(repeat, blocks_ref[...], preferred_element_type=F32)
    rows = jnp.where(iota2(rows.shape, 0) % BLK == iota2(rows.shape, 1) // BLK, rows, 0.0).astype(BF16)
    spread = (iota2((AREA, width), 0) % BLK == iota2((AREA, width), 1) % BLK).astype(BF16)
    density[...] = jnp.dot(rows, spread, preferred_element_type=F32).reshape(nblocks, BLK, width)
    column = iota2((BLK, width), 1) // BLK
    for t in range(ntiles):
        line = jnp.zeros((BLK, width), F32)
        for s in range(listed_sources):
            line = line + jnp.where(column == src_ref[t, s], density[block_ref[t, s]], 0.0)
        mix_ref[t * BLK:(t + 1) * BLK, :] = line.astype(BF16)

    pair = lax.axis_index("pair")
    plane, core = pair // CORES, pair % CORES
    planes, per_owner, _ = mine_ref.shape
    for k in range(planes):
        held[k * per_owner:(k + 1) * per_owner, :] = mine_ref[k].astype(F32)
        held[(planes + k) * per_owner:(planes + k + 1) * per_owner, :] = theirs_ref[k].astype(F32)
    pick = (iota2((AREA, AREA), 0) % BLK == iota2((AREA, AREA), 1) % BLK).astype(F32)
    place = (iota2((AREA, AREA), 0) // BLK == iota2((AREA, AREA), 1) // BLK).astype(BF16)
    same = iota2((AREA, AREA), 0) // BLK == iota2((AREA, AREA), 1) % BLK
    for t in range(ntiles):
        k, flip = plane ^ (t // CORES), core ^ (t % CORES)
        row = (flip * planes + k) * per_owner + jnp.clip(listed_ref[0, t, 0] - t * per_owner, 0, per_owner - 1)
        chosen = (pick * held[pl.ds(row, 1), :]).astype(BF16)
        full = jnp.dot(chosen, place, preferred_element_type=F32)
        wide_ref[t] = jnp.where(same, full, 0.0).astype(BF16)


NT_DIMS = (((1,), (1,)), ((), ()))


def half_rows(tiles, mix, mixed, halves):
    ntiles = halves.shape[0]
    rows, cols = iota2((AREA, AREA), 0), iota2((AREA, AREA), 1)
    swap = ((rows % BLK == cols // BLK) & (rows // BLK == cols % BLK)).astype(BF16)
    for k in range(ntiles):
        block = jnp.concatenate([ref[:, k * AREA:(k + 1) * AREA] for ref in tiles], axis=0)
        turned = lax.dot_general(swap, block, NT_DIMS, preferred_element_type=F32).astype(BF16)
        for n in range(BLK):
            mixed[n, k * BLK:(k + 1) * BLK, :] = turned[n * BLK:(n + 1) * BLK, :]
    for n in range(BLK):
        half = jnp.dot(mix, mixed[n], preferred_element_type=F32).astype(BF16)
        for t in range(ntiles):
            halves[t, n * BLK:(n + 1) * BLK, :] = half[t * BLK:(t + 1) * BLK, :]


def k_own_body(tile_ref, mix_ref, wide_ref, out_ref, mixed, halves):
    half_rows((tile_ref,), mix_ref[...], mixed, halves)
    for t in range(wide_ref.shape[0]):
        out_ref[:, t * AREA:(t + 1) * AREA] = lax.dot_general(
            halves[t], wide_ref[t], (((0,), (1,)), ((), ())), preferred_element_type=F32
        ).astype(BF16)


def k_moved_body(inner_ref, outer_ref, mix_ref, wide_ref, out_ref, mixed, halves):
    half_rows((inner_ref, outer_ref), mix_ref[...], mixed, halves)
    for t in range(wide_ref.shape[0]):
        out_ref[t * AREA:(t + 1) * AREA, :] = jnp.dot(
            wide_ref[t], halves[t], preferred_element_type=F32
        ).astype(BF16)


def packed(top, bottom):
    half = top.shape[0] // 2
    return jnp.concatenate([top[:half], top[half:], bottom[:half], bottom[half:]], axis=1)


def arranged(top, bottom):
    cut = far_cut(top.shape[1])
    return jnp.concatenate([packed(top[:, :cut], bottom[:, :cut]), packed(top[:, cut:], bottom[:, cut:])], axis=1)


def far_cut(aux):
    return aux // 256 * 256 or aux // 2


def dot_rows(left, right):
    return lax.dot_general(left, right, NT_DIMS, preferred_element_type=F32)


def near_body(o_ref, p_ref, k_ref, out_ref):
    right = k_ref[...]
    out_ref[...] = arranged(dot_rows(o_ref[...], right), dot_rows(p_ref[...], right))


def place_of():
    plane, red = lax.axis_index("pair") // CORES, lax.axis_index("red")
    near = plane < 2
    return jnp.where(near, plane, 3 - plane), jnp.where(near, red, 3 - red)


def early_body(o_ref, p_ref, e_ref, f_ref, g_ref, kt_ref, near_ref, own_ref, s1, s2, s3, held_ref, terms):
    aux = o_ref.shape[0]
    right = kt_ref[...]
    top = jnp.dot(o_ref[...], right, preferred_element_type=F32)
    bottom = jnp.dot(p_ref[...], right, preferred_element_type=F32)
    terms[0] = near_ref[...]
    terms[1] = arranged(top[:, aux:], bottom[:, aux:])
    terms[2] = arranged(top[:, :aux], bottom[:, :aux])
    inner = kt_ref[:, :aux]
    lower = jnp.concatenate([f_ref[...], g_ref[...]], axis=0)
    terms[3] = arranged(
        jnp.dot(e_ref[...], inner, preferred_element_type=F32), jnp.dot(lower, inner, preferred_element_type=F32)
    )
    plane, place = place_of()
    hub = plane == 1

    def term_for(column):
        return jnp.where(hub, jnp.where(column < 2, 1 - column, column), jnp.minimum(column, 1))

    mine = hub & (place < 3) | (plane == 0) & (place < 2)
    own_ref[...] = jnp.where(mine, terms[term_for(place)], 0.0)
    for d, out in zip((1, 2, 3), (s1, s2, s3)):
        out[...] = terms[term_for(place ^ d)].astype(BF16)
    held_ref[...] = terms[3].astype(BF16)


LATE = ((2, 0, None, 1), (0, 2, None, None), (None, None, 0, 2), (None, None, 2, None))
LATE_TO = {0: (1, 3), 1: (0, 2), 2: (0, 3)}


def by_place(place, values):
    chosen = jnp.int32(values[3] or 0)
    for at in (2, 1, 0):
        chosen = jnp.where(place == at, values[at] or 0, chosen)
    return chosen


def late_body(k_ref, o_ref, p_ref, e_ref, f_ref, g_ref, held_ref, own_ref, s1, s2, s3, s4, terms):
    right = k_ref[...]
    plane, place = place_of()
    lower = jnp.concatenate([f_ref[...], g_ref[...]], axis=0)
    near = packed(dot_rows(o_ref[...], right), dot_rows(p_ref[...], right))
    own_ref[...] = jnp.where((plane == 1) & (place == 3), near, 0.0)
    terms[0] = near.astype(BF16)
    terms[1] = held_ref[...]
    terms[2] = packed(dot_rows(e_ref[...], right), dot_rows(lower, right)).astype(BF16)
    for sent, out in zip(LATE, (s1, s2, s3, s4)):
        out[...] = terms[by_place(place, sent)]


def last_body(k_ref, o_ref, p_ref, e_ref, f_ref, g_ref, held_ref, *refs):
    first, (own_ref, s1, s2, s3, s4, terms, own_part, t1, t2, t3, t4) = refs[:5], refs[5:]
    parts = (own_part, t1, t2, t3, t4)
    late_body(k_ref, o_ref, p_ref, e_ref, f_ref, g_ref, held_ref, *parts, terms)
    cut = first[0].shape[1]
    for out, before, part in zip((own_ref, s1, s2, s3, s4), first, parts):
        out[:, :cut] = before[...]
        out[:, cut:] = part[...]


def sum_body(*refs):
    values, sides = refs[:-2], refs[-2:]
    width = sides[0].shape[1]
    cut = far_cut(width // 2)
    for at, side in enumerate(sides):
        for start, size, to in ((at * 2 * cut, 2 * cut, 0), (4 * cut + at * (width - 2 * cut), width - 2 * cut, 2 * cut)):
            total = values[0][:, start:start + size]
            for value in values[1:]:
                total = total + value[:, start:start + size].astype(F32)
            side[:, to:to + size] = total


def join_body(kept_ref, other_ref, out_ref):
    first = lax.axis_index("pair") % CORES == 0
    kept, other = kept_ref[...], other_ref[...]
    left, right = jnp.where(first, kept, other), jnp.where(first, other, kept)
    half, aux = left.shape[0], left.shape[1] // 2
    cut = far_cut(aux)
    for at in range(2):
        pieces = [
            piece
            for side in (left, right)
            for piece in (side[:, at * cut:(at + 1) * cut], side[:, 2 * cut + at * (aux - cut):2 * cut + (at + 1) * (aux - cut)])
        ]
        out_ref[at * half:(at + 1) * half, :] = jnp.concatenate(pieces, axis=1)


def call(body, outs, ins, scratch=(), smem=0, name=None):
    return pl.pallas_call(
        body,
        out_shape=outs,
        in_specs=[pl.BlockSpec(memory_space=pltpu.SMEM)] * smem
        + [pl.BlockSpec(memory_space=pltpu.VMEM)] * (len(ins) - smem),
        out_specs=jax.tree.map(lambda _: pl.BlockSpec(memory_space=pltpu.VMEM), outs),
        scratch_shapes=list(scratch),
        compiler_params=pltpu.CompilerParams(vmem_limit_bytes=VMEM_BYTES),
        cost_estimate=pl.CostEstimate(
            flops=1, transcendentals=0, bytes_accessed=1
        ),
        name=name,
    )(*ins)


def shaped(*shape, dtype=BF16):
    return jax.ShapeDtypeStruct(shape, dtype)


def hub_plan(three_center, occ_src, occ_block, occ_blocks, virt_block, virt_blocks):
    aux, ntiles, area = three_center.shape
    depth = ntiles * area

    def along_z(moves):
        return [(CORES * a + c, CORES * b + c) for a, b in moves for c in range(CORES)]

    core_swap = [(i, i ^ 1) for i in range(8)]
    both = ("pair", "red")

    def everywhere(moves):
        full = list(moves) + [((3 - a, 3 - g), (3 - b, 3 - h)) for (a, g), (b, h) in moves]
        return [((CORES * a + c) * 4 + g, (CORES * b + c) * 4 + h) for (a, g), (b, h) in full for c in range(CORES)]

    after = lax.optimization_barrier

    def scratch_for(count):
        return [pltpu.VMEM((BLK, ntiles * BLK, count), BF16), pltpu.VMEM((ntiles, area, count), BF16)]

    from_planes = [virt_blocks] + [
        lax.ppermute(virt_blocks, "pair", along_z([(a, a ^ k) for a in range(4)])) for k in (1, 2, 3)
    ]
    tiles = three_center.reshape(aux, depth)
    *from_planes, tiles = after((*from_planes, tiles))
    inner = lax.ppermute(tiles, "pair", along_z([(1, 2), (2, 1)]))
    mine = jnp.concatenate(from_planes)
    theirs = lax.ppermute(mine, "pair", core_swap)
    partner = lax.ppermute(tiles, "pair", core_swap)
    theirs, tiles = after((theirs, tiles))
    outer = lax.ppermute(tiles, "pair", along_z([(0, 1), (1, 0), (2, 3), (3, 2)]))
    mix, wide = call(
        prep_body,
        [shaped(ntiles * BLK, ntiles * BLK), shaped(ntiles, area, area)],
        [occ_src, occ_block, virt_block, occ_blocks, mine, theirs],
        [
            pltpu.VMEM((occ_blocks.shape[0], BLK, ntiles * BLK), F32),
            pltpu.VMEM((CORES * mine.shape[0] * mine.shape[1], area), F32),
        ],
        smem=3, name="prep",
    )
    partner, wide, tiles = after((partner, wide, tiles))
    k_own = call(k_own_body, shaped(aux, depth), [tiles, mix, wide], scratch_for(aux), name="k_own")
    cut = far_cut(aux)
    far = [lax.ppermute(part, "pair", along_z([(0, 2), (3, 1)])) for part in (k_own[:cut], k_own[cut:])]
    term = (aux // 2, 4 * aux)
    near = call(near_body, shaped(*term, dtype=F32), [tiles, partner, k_own], name="near")
    outer, inner, near = after((outer, inner, near))

    outer_partner = [lax.ppermute(outer[at:at + aux // 2], "pair", core_swap) for at in (0, aux // 2)]
    k_moved = call(
        k_moved_body, shaped(depth, 2 * aux), [inner, outer, mix, wide], scratch_for(2 * aux), name="k_moved"
    )
    own_early, *sent, held = call(
        early_body,
        [shaped(*term, dtype=F32)] + [shaped(*term)] * 4,
        [tiles, partner, outer, *outer_partner, k_moved, near],
        [pltpu.VMEM((4, *term), F32)],
        name="early",
    )
    arrived = []
    for d, value in reversed(list(zip((1, 2, 3), sent))):
        moves = [((1, g), (1, g ^ d)) for g in range(4) if g ^ d != 3]
        moves += [((0, g), (0, g ^ d)) for g in range(4) if g ^ d < 2]
        moves += [((1, 3 ^ d), (0, 2))]
        arrived.append(lax.ppermute(value, both, everywhere(moves)))

    far[0], held = after((far[0], held))
    part = (aux // 2, 4 * cut)
    first_part = call(
        late_body,
        [shaped(*part, dtype=F32)] + [shaped(*part)] * 4,
        [far[0], tiles, partner, outer, *outer_partner, held[:, :4 * cut]],
        [pltpu.VMEM((3, *part), BF16)],
        name="late",
    )
    far[1], *first_part = after((far[1], *first_part))
    rest = (aux // 2, 4 * (aux - cut))
    own_late, *late_sent = call(
        last_body,
        [shaped(*term, dtype=F32)] + [shaped(*term)] * 4,
        [far[1], tiles, partner, outer, *outer_partner, held[:, 4 * cut:], *first_part],
        [pltpu.VMEM((3, *rest), BF16), pltpu.VMEM(rest, F32)] + [pltpu.VMEM(rest, BF16)] * 4,
        name="last",
    )
    for sources, value in zip(LATE, late_sent):
        moves = [((1, g), LATE_TO[what]) for g, what in enumerate(sources) if what is not None]
        arrived.append(lax.ppermute(value, both, everywhere(moves)))
    mine, yours = call(
        sum_body, [shaped(aux // 2, 2 * aux, dtype=F32)] * 2, [own_early, own_late, *arrived], name="sum"
    )
    other = lax.ppermute(yours, "pair", core_swap)
    return call(join_body, shaped(aux, 2 * aux, dtype=F32), [mine, other], name="join")


def solution(mesh):
    placed = (
        P("pair", "red", None),
        P("red", None),
        P("red", None),
        P("red", None),
        P("red", None, None),
        P("red", "pair", None),
    )
    line = mesh.shape["pair"] == 4 * CORES and mesh.shape["red"] == 4

    def shards(three_center, occ_src, occ_block, occ_blocks, virt_block, virt_blocks):
        owned = virt_block.shape[2] == 1 and virt_block.shape[1] == mesh.shape["pair"]
        plan = hub_plan if line and owned and three_center.shape[0] % 32 == 0 else gather_plan
        return plan(three_center, occ_src, occ_block, occ_blocks, virt_block, virt_blocks)

    return jax.shard_map(shards, mesh=mesh, in_specs=placed, out_specs=P("pair", "red"), check_vma=False)
```

```python
import functools

import jax
import jax.numpy as jnp
from jax import lax
from jax.experimental import pallas as pl
from jax.experimental.pallas import tpu as pltpu
from jax.sharding import PartitionSpec as P

BLK = 16
AREA = BLK * BLK
VMEM_BYTES = 24 * 1024 * 1024
CORES = 2
BF16 = jnp.bfloat16
F32 = jnp.float32


def mixing_of(occ_src, occ_block, occ_blocks, ntiles):
    nblocks = occ_blocks.shape[0]
    block_hot = (occ_block[:, :, None] == jnp.arange(nblocks, dtype=jnp.int32)).astype(BF16)
    picked = jnp.einsum("tsb,bk->tsk", block_hot, occ_blocks, preferred_element_type=F32).astype(BF16)
    source_hot = (occ_src[:, :, None] == jnp.arange(ntiles, dtype=jnp.int32)).astype(BF16)
    mixing = jnp.einsum("tsk,tsa->tka", source_hot, picked, preferred_element_type=F32).astype(BF16)
    return mixing.reshape(ntiles, ntiles, BLK, BLK)


def gather_plan(three_center, occ_src, occ_block, occ_blocks, virt_block, virt_blocks):
    aux_rows, ntiles, area = three_center.shape
    tpd = virt_block.shape[2]
    mixing = mixing_of(occ_src, occ_block, occ_blocks, ntiles)
    blocks = three_center.reshape(aux_rows, ntiles, BLK, BLK)
    half = jnp.einsum("tkml,pkln->ptmn", mixing, blocks, preferred_element_type=F32).astype(BF16)
    all_blocks = lax.all_gather(virt_blocks[0], "pair", axis=0, tiled=True)
    listed = virt_block[0].reshape(ntiles // tpd, tpd, tpd)
    block_hot = (listed[..., None] == jnp.arange(all_blocks.shape[0], dtype=jnp.int32)).astype(BF16)
    picked = jnp.einsum("oijb,bk->oijk", block_hot, all_blocks, preferred_element_type=F32).astype(BF16)
    picked = picked.reshape(ntiles // tpd, tpd, tpd, BLK, BLK)
    grouped = half.reshape(aux_rows, ntiles // tpd, tpd, BLK, BLK)
    kernel = jnp.einsum("pojml,oijln->poimn", grouped, picked, preferred_element_type=F32)
    kernel = kernel.reshape(aux_rows, ntiles, area).astype(BF16)
    piece = lax.all_gather(kernel, "pair", axis=0, tiled=True)
    partial_value = lax.dot_general(
        three_center.reshape(aux_rows, ntiles * area),
        piece.reshape(piece.shape[0], ntiles * area),
        (((1,), (1,)), ((), ())),
        preferred_element_type=F32,
    )
    return lax.psum_scatter(partial_value, "red", scatter_dimension=1, tiled=True)


def iota2(shape, dim):
    return lax.broadcasted_iota(jnp.int32, shape, dim)


def prep_body(src_ref, block_ref, listed_ref, blocks_ref, mine_ref, theirs_ref, mix_ref, wide_ref, density, held):
    nblocks = blocks_ref.shape[0]
    ntiles, listed_sources = src_ref.shape
    width = ntiles * BLK
    repeat = (iota2((nblocks * BLK, nblocks), 0) // BLK == iota2((nblocks * BLK, nblocks), 1)).astype(BF16)
    rows = jnp.dot(repeat, blocks_ref[...], preferred_element_type=F32)
    rows = jnp.where(iota2(rows.shape, 0) % BLK == iota2(rows.shape, 1) // BLK, rows, 0.0).astype(BF16)
    spread = (iota2((AREA, width), 0) % BLK == iota2((AREA, width), 1) % BLK).astype(BF16)
    density[...] = jnp.dot(rows, spread, preferred_element_type=F32).reshape(nblocks, BLK, width)
    column = iota2((BLK, width), 1) // BLK
    for t in range(ntiles):
        line = jnp.zeros((BLK, width), F32)
        for s in range(listed_sources):
            line = line + jnp.where(column == src_ref[t, s], density[block_ref[t, s]], 0.0)
        mix_ref[t * BLK:(t + 1) * BLK, :] = line.astype(BF16)

    pair = lax.axis_index("pair")
    plane, core = pair // CORES, pair % CORES
    planes, per_owner, _ = mine_ref.shape
    for k in range(planes):
        held[k * per_owner:(k + 1) * per_owner, :] = mine_ref[k].astype(F32)
        held[(planes + k) * per_owner:(planes + k + 1) * per_owner, :] = theirs_ref[k].astype(F32)
    pick = (iota2((AREA, AREA), 0) % BLK == iota2((AREA, AREA), 1) % BLK).astype(F32)
    place = (iota2((AREA, AREA), 0) // BLK == iota2((AREA, AREA), 1) // BLK).astype(BF16)
    same = iota2((AREA, AREA), 0) // BLK == iota2((AREA, AREA), 1) % BLK
    for t in range(ntiles):
        k, flip = plane ^ (t // CORES), core ^ (t % CORES)
        row = (flip * planes + k) * per_owner + jnp.clip(listed_ref[0, t, 0] - t * per_owner, 0, per_owner - 1)
        chosen = (pick * held[pl.ds(row, 1), :]).astype(BF16)
        full = jnp.dot(chosen, place, preferred_element_type=F32)
        wide_ref[t] = jnp.where(same, full, 0.0).astype(BF16)


NT_DIMS = (((1,), (1,)), ((), ()))


def half_rows(tiles, mix, mixed, halves):
    ntiles = halves.shape[0]
    rows, cols = iota2((AREA, AREA), 0), iota2((AREA, AREA), 1)
    swap = ((rows % BLK == cols // BLK) & (rows // BLK == cols % BLK)).astype(BF16)
    for k in range(ntiles):
        block = jnp.concatenate([ref[:, k * AREA:(k + 1) * AREA] for ref in tiles], axis=0)
        turned = lax.dot_general(swap, block, NT_DIMS, preferred_element_type=F32).astype(BF16)
        for n in range(BLK):
            mixed[n, k * BLK:(k + 1) * BLK, :] = turned[n * BLK:(n + 1) * BLK, :]
    for n in range(BLK):
        half = jnp.dot(mix, mixed[n], preferred_element_type=F32).astype(BF16)
        for t in range(ntiles):
            halves[t, n * BLK:(n + 1) * BLK, :] = half[t * BLK:(t + 1) * BLK, :]


def k_own_body(tile_ref, mix_ref, wide_ref, out_ref, mixed, halves):
    half_rows((tile_ref,), mix_ref[...], mixed, halves)
    for t in range(wide_ref.shape[0]):
        out_ref[:, t * AREA:(t + 1) * AREA] = lax.dot_general(
            halves[t], wide_ref[t], (((0,), (1,)), ((), ())), preferred_element_type=F32
        ).astype(BF16)


def k_moved_body(inner_ref, outer_ref, mix_ref, wide_ref, out_ref, mixed, halves):
    half_rows((inner_ref, outer_ref), mix_ref[...], mixed, halves)
    for t in range(wide_ref.shape[0]):
        out_ref[t * AREA:(t + 1) * AREA, :] = jnp.dot(
            wide_ref[t], halves[t], preferred_element_type=F32
        ).astype(BF16)


def packed(top, bottom):
    half = top.shape[0] // 2
    return jnp.concatenate([top[:half], top[half:], bottom[:half], bottom[half:]], axis=1)


def arranged(top, bottom):
    cut = far_cut(top.shape[1])
    return jnp.concatenate([packed(top[:, :cut], bottom[:, :cut]), packed(top[:, cut:], bottom[:, cut:])], axis=1)


def far_cut(aux):
    return aux // 256 * 256 or aux // 2


def dot_rows(left, right):
    return lax.dot_general(left, right, NT_DIMS, preferred_element_type=F32)


def near_body(o_ref, p_ref, k_ref, out_ref):
    right = k_ref[...]
    out_ref[...] = arranged(dot_rows(o_ref[...], right), dot_rows(p_ref[...], right))


def place_of():
    plane, red = lax.axis_index("pair") // CORES, lax.axis_index("red")
    near = plane < 2
    return jnp.where(near, plane, 3 - plane), jnp.where(near, red, 3 - red)


def early_body(o_ref, p_ref, e_ref, f_ref, g_ref, kt_ref, near_ref, own_ref, s1, s2, s3, held_ref, terms):
    aux = o_ref.shape[0]
    right = kt_ref[...]
    top = jnp.dot(o_ref[...], right, preferred_element_type=F32)
    bottom = jnp.dot(p_ref[...], right, preferred_element_type=F32)
    terms[0] = near_ref[...]
    terms[1] = arranged(top[:, aux:], bottom[:, aux:])
    terms[2] = arranged(top[:, :aux], bottom[:, :aux])
    inner = kt_ref[:, :aux]
    lower = jnp.concatenate([f_ref[...], g_ref[...]], axis=0)
    terms[3] = arranged(
        jnp.dot(e_ref[...], inner, preferred_element_type=F32), jnp.dot(lower, inner, preferred_element_type=F32)
    )
    plane, place = place_of()
    hub = plane == 1

    def term_for(column):
        return jnp.where(hub, jnp.where(column < 2, 1 - column, column), jnp.minimum(column, 1))

    mine = hub & (place < 3) | (plane == 0) & (place < 2)
    own_ref[...] = jnp.where(mine, terms[term_for(place)], 0.0)
    for d, out in zip((1, 2, 3), (s1, s2, s3)):
        out[...] = terms[term_for(place ^ d)].astype(BF16)
    held_ref[...] = terms[3].astype(BF16)


LATE = ((2, 0, None, 1), (0, 2, None, None), (None, None, 0, 2), (None, None, 2, None))
LATE_TO = {0: (1, 3), 1: (0, 2), 2: (0, 3)}


def by_place(place, values):
    chosen = jnp.int32(values[3] or 0)
    for at in (2, 1, 0):
        chosen = jnp.where(place == at, values[at] or 0, chosen)
    return chosen


def late_body(k_ref, o_ref, p_ref, e_ref, f_ref, g_ref, held_ref, own_ref, s1, s2, s3, s4, terms):
    right = k_ref[...]
    plane, place = place_of()
    lower = jnp.concatenate([f_ref[...], g_ref[...]], axis=0)
    near = packed(dot_rows(o_ref[...], right), dot_rows(p_ref[...], right))
    own_ref[...] = jnp.where((plane == 1) & (place == 3), near, 0.0)
    terms[0] = near.astype(BF16)
    terms[1] = held_ref[...]
    terms[2] = packed(dot_rows(e_ref[...], right), dot_rows(lower, right)).astype(BF16)
    for sent, out in zip(LATE, (s1, s2, s3, s4)):
        out[...] = terms[by_place(place, sent)]


def last_body(k_ref, o_ref, p_ref, e_ref, f_ref, g_ref, held_ref, *refs):
    first, (own_ref, s1, s2, s3, s4, terms, own_part, t1, t2, t3, t4) = refs[:5], refs[5:]
    parts = (own_part, t1, t2, t3, t4)
    late_body(k_ref, o_ref, p_ref, e_ref, f_ref, g_ref, held_ref, *parts, terms)
    cut = first[0].shape[1]
    for out, before, part in zip((own_ref, s1, s2, s3, s4), first, parts):
        out[:, :cut] = before[...]
        out[:, cut:] = part[...]


def sum_body(*refs):
    values, sides = refs[:-2], refs[-2:]
    width = sides[0].shape[1]
    cut = far_cut(width // 2)
    for at, side in enumerate(sides):
        for start, size, to in ((at * 2 * cut, 2 * cut, 0), (4 * cut + at * (width - 2 * cut), width - 2 * cut, 2 * cut)):
            total = values[0][:, start:start + size]
            for value in values[1:]:
                total = total + value[:, start:start + size].astype(F32)
            side[:, to:to + size] = total


def join_body(kept_ref, other_ref, out_ref):
    first = lax.axis_index("pair") % CORES == 0
    kept, other = kept_ref[...], other_ref[...]
    left, right = jnp.where(first, kept, other), jnp.where(first, other, kept)
    half, aux = left.shape[0], left.shape[1] // 2
    cut = far_cut(aux)
    for at in range(2):
        pieces = [
            piece
            for side in (left, right)
            for piece in (side[:, at * cut:(at + 1) * cut], side[:, 2 * cut + at * (aux - cut):2 * cut + (at + 1) * (aux - cut)])
        ]
        out_ref[at * half:(at + 1) * half, :] = jnp.concatenate(pieces, axis=1)


def call(body, outs, ins, scratch=(), smem=0, name=None):
    return pl.pallas_call(
        body,
        out_shape=outs,
        in_specs=[pl.BlockSpec(memory_space=pltpu.SMEM)] * smem
        + [pl.BlockSpec(memory_space=pltpu.VMEM)] * (len(ins) - smem),
        out_specs=jax.tree.map(lambda _: pl.BlockSpec(memory_space=pltpu.VMEM), outs),
        scratch_shapes=list(scratch),
        compiler_params=pltpu.CompilerParams(vmem_limit_bytes=VMEM_BYTES),
        cost_estimate=pl.CostEstimate(
            flops=1, transcendentals=0, bytes_accessed=1
        ),
        name=name,
    )(*ins)


def shaped(*shape, dtype=BF16):
    return jax.ShapeDtypeStruct(shape, dtype)


def hub_plan(three_center, occ_src, occ_block, occ_blocks, virt_block, virt_blocks):
    aux, ntiles, area = three_center.shape
    depth = ntiles * area

    def along_z(moves):
        return [(CORES * a + c, CORES * b + c) for a, b in moves for c in range(CORES)]

    core_swap = [(i, i ^ 1) for i in range(8)]
    both = ("pair", "red")

    def everywhere(moves):
        full = list(moves) + [((3 - a, 3 - g), (3 - b, 3 - h)) for (a, g), (b, h) in moves]
        return [((CORES * a + c) * 4 + g, (CORES * b + c) * 4 + h) for (a, g), (b, h) in full for c in range(CORES)]

    after = lax.optimization_barrier

    def scratch_for(count):
        return [pltpu.VMEM((BLK, ntiles * BLK, count), BF16), pltpu.VMEM((ntiles, area, count), BF16)]

    from_planes = [virt_blocks] + [
        lax.ppermute(virt_blocks, "pair", along_z([(a, a ^ k) for a in range(4)])) for k in (1, 2, 3)
    ]
    tiles = three_center.reshape(aux, depth)
    *from_planes, tiles = after((*from_planes, tiles))
    inner = lax.ppermute(tiles, "pair", along_z([(1, 2), (2, 1)]) + [(0, 1), (1, 0), (6, 7), (7, 6)])
    mine = jnp.concatenate(from_planes)
    theirs = lax.ppermute(mine, "pair", core_swap)
    partner = lax.ppermute(tiles, "pair", core_swap)
    theirs, tiles = after((theirs, tiles))
    outer = lax.ppermute(tiles, "pair", along_z([(0, 1), (1, 0), (2, 3), (3, 2)]))
    mix, wide = call(
        prep_body,
        [shaped(ntiles * BLK, ntiles * BLK), shaped(ntiles, area, area)],
        [occ_src, occ_block, virt_block, occ_blocks, mine, theirs],
        [
            pltpu.VMEM((occ_blocks.shape[0], BLK, ntiles * BLK), F32),
            pltpu.VMEM((CORES * mine.shape[0] * mine.shape[1], area), F32),
        ],
        smem=3, name="prep",
    )
    partner, wide, tiles = after((partner, wide, tiles))
    k_own = call(k_own_body, shaped(aux, depth), [tiles, mix, wide], scratch_for(aux), name="k_own")
    cut = far_cut(aux)
    far = [lax.ppermute(part, "pair", along_z([(0, 2), (3, 1)])) for part in (k_own[:cut], k_own[cut:])]
    term = (aux // 2, 4 * aux)
    near = call(near_body, shaped(*term, dtype=F32), [tiles, partner, k_own], name="near")
    outer, inner, near = after((outer, inner, near))

    outer_partner = [lax.ppermute(outer[at:at + aux // 2], "pair", core_swap) for at in (0, aux // 2)]
    k_moved = call(
        k_moved_body, shaped(depth, 2 * aux), [inner, outer, mix, wide], scratch_for(2 * aux), name="k_moved"
    )
    own_early, *sent, held = call(
        early_body,
        [shaped(*term, dtype=F32)] + [shaped(*term)] * 4,
        [tiles, partner, outer, *outer_partner, k_moved, near],
        [pltpu.VMEM((4, *term), F32)],
        name="early",
    )
    arrived = []
    for d, value in reversed(list(zip((1, 2, 3), sent))):
        moves = [((1, g), (1, g ^ d)) for g in range(4) if g ^ d != 3]
        moves += [((0, g), (0, g ^ d)) for g in range(4) if g ^ d < 2]
        moves += [((1, 3 ^ d), (0, 2))]
        arrived.append(lax.ppermute(value, both, everywhere(moves)))

    far[0], held = after((far[0], held))
    part = (aux // 2, 4 * cut)
    first_part = call(
        late_body,
        [shaped(*part, dtype=F32)] + [shaped(*part)] * 4,
        [far[0], tiles, partner, outer, *outer_partner, held[:, :4 * cut]],
        [pltpu.VMEM((3, *part), BF16)],
        name="late",
    )
    far[1], *first_part = after((far[1], *first_part))
    rest = (aux // 2, 4 * (aux - cut))
    own_late, *late_sent = call(
        last_body,
        [shaped(*term, dtype=F32)] + [shaped(*term)] * 4,
        [far[1], tiles, partner, outer, *outer_partner, held[:, 4 * cut:], *first_part],
        [pltpu.VMEM((3, *rest), BF16), pltpu.VMEM(rest, F32)] + [pltpu.VMEM(rest, BF16)] * 4,
        name="last",
    )
    for sources, value in zip(LATE, late_sent):
        moves = [((1, g), LATE_TO[what]) for g, what in enumerate(sources) if what is not None]
        arrived.append(lax.ppermute(value, both, everywhere(moves)))
    mine, yours = call(
        sum_body, [shaped(aux // 2, 2 * aux, dtype=F32)] * 2, [own_early, own_late, *arrived], name="sum"
    )
    other = lax.ppermute(yours, "pair", core_swap)
    return call(join_body, shaped(aux, 2 * aux, dtype=F32), [mine, other], name="join")


def solution(mesh):
    placed = (
        P("pair", "red", None),
        P("red", None),
        P("red", None),
        P("red", None),
        P("red", None, None),
        P("red", "pair", None),
    )
    line = mesh.shape["pair"] == 4 * CORES and mesh.shape["red"] == 4

    def shards(three_center, occ_src, occ_block, occ_blocks, virt_block, virt_blocks):
        owned = virt_block.shape[2] == 1 and virt_block.shape[1] == mesh.shape["pair"]
        plan = hub_plan if line and owned and three_center.shape[0] % 32 == 0 else gather_plan
        return plan(three_center, occ_src, occ_block, occ_blocks, virt_block, virt_blocks)

    return jax.shard_map(shards, mesh=mesh, in_specs=placed, out_specs=P("pair", "red"), check_vma=False)
```

```python
import functools

import jax
import jax.numpy as jnp
from jax import lax
from jax.experimental import pallas as pl
from jax.experimental.pallas import tpu as pltpu
from jax.sharding import PartitionSpec as P

BLK = 16
AREA = BLK * BLK
VMEM_BYTES = 24 * 1024 * 1024
CORES = 2
BF16 = jnp.bfloat16
F32 = jnp.float32


def mixing_of(occ_src, occ_block, occ_blocks, ntiles):
    nblocks = occ_blocks.shape[0]
    block_hot = (occ_block[:, :, None] == jnp.arange(nblocks, dtype=jnp.int32)).astype(BF16)
    picked = jnp.einsum("tsb,bk->tsk", block_hot, occ_blocks, preferred_element_type=F32).astype(BF16)
    source_hot = (occ_src[:, :, None] == jnp.arange(ntiles, dtype=jnp.int32)).astype(BF16)
    mixing = jnp.einsum("tsk,tsa->tka", source_hot, picked, preferred_element_type=F32).astype(BF16)
    return mixing.reshape(ntiles, ntiles, BLK, BLK)


def gather_plan(three_center, occ_src, occ_block, occ_blocks, virt_block, virt_blocks):
    aux_rows, ntiles, area = three_center.shape
    tpd = virt_block.shape[2]
    mixing = mixing_of(occ_src, occ_block, occ_blocks, ntiles)
    blocks = three_center.reshape(aux_rows, ntiles, BLK, BLK)
    half = jnp.einsum("tkml,pkln->ptmn", mixing, blocks, preferred_element_type=F32).astype(BF16)
    all_blocks = lax.all_gather(virt_blocks[0], "pair", axis=0, tiled=True)
    listed = virt_block[0].reshape(ntiles // tpd, tpd, tpd)
    block_hot = (listed[..., None] == jnp.arange(all_blocks.shape[0], dtype=jnp.int32)).astype(BF16)
    picked = jnp.einsum("oijb,bk->oijk", block_hot, all_blocks, preferred_element_type=F32).astype(BF16)
    picked = picked.reshape(ntiles // tpd, tpd, tpd, BLK, BLK)
    grouped = half.reshape(aux_rows, ntiles // tpd, tpd, BLK, BLK)
    kernel = jnp.einsum("pojml,oijln->poimn", grouped, picked, preferred_element_type=F32)
    kernel = kernel.reshape(aux_rows, ntiles, area).astype(BF16)
    piece = lax.all_gather(kernel, "pair", axis=0, tiled=True)
    partial_value = lax.dot_general(
        three_center.reshape(aux_rows, ntiles * area),
        piece.reshape(piece.shape[0], ntiles * area),
        (((1,), (1,)), ((), ())),
        preferred_element_type=F32,
    )
    return lax.psum_scatter(partial_value, "red", scatter_dimension=1, tiled=True)


def iota2(shape, dim):
    return lax.broadcasted_iota(jnp.int32, shape, dim)


def prep_body(src_ref, block_ref, listed_ref, blocks_ref, mine_ref, theirs_ref, mix_ref, wide_ref, density, held):
    nblocks = blocks_ref.shape[0]
    ntiles, listed_sources = src_ref.shape
    width = ntiles * BLK
    repeat = (iota2((nblocks * BLK, nblocks), 0) // BLK == iota2((nblocks * BLK, nblocks), 1)).astype(BF16)
    rows = jnp.dot(repeat, blocks_ref[...], preferred_element_type=F32)
    rows = jnp.where(iota2(rows.shape, 0) % BLK == iota2(rows.shape, 1) // BLK, rows, 0.0).astype(BF16)
    spread = (iota2((AREA, width), 0) % BLK == iota2((AREA, width), 1) % BLK).astype(BF16)
    density[...] = jnp.dot(rows, spread, preferred_element_type=F32).reshape(nblocks, BLK, width)
    column = iota2((BLK, width), 1) // BLK
    for t in range(ntiles):
        line = jnp.zeros((BLK, width), F32)
        for s in range(listed_sources):
            line = line + jnp.where(column == src_ref[t, s], density[block_ref[t, s]], 0.0)
        mix_ref[t * BLK:(t + 1) * BLK, :] = line.astype(BF16)

    pair = lax.axis_index("pair")
    plane, core = pair // CORES, pair % CORES
    planes, per_owner, _ = mine_ref.shape
    for k in range(planes):
        held[k * per_owner:(k + 1) * per_owner, :] = mine_ref[k].astype(F32)
        held[(planes + k) * per_owner:(planes + k + 1) * per_owner, :] = theirs_ref[k].astype(F32)
    pick = (iota2((AREA, AREA), 0) % BLK == iota2((AREA, AREA), 1) % BLK).astype(F32)
    place = (iota2((AREA, AREA), 0) // BLK == iota2((AREA, AREA), 1) // BLK).astype(BF16)
    same = iota2((AREA, AREA), 0) // BLK == iota2((AREA, AREA), 1) % BLK
    for t in range(ntiles):
        k, flip = plane ^ (t // CORES), core ^ (t % CORES)
        row = (flip * planes + k) * per_owner + jnp.clip(listed_ref[0, t, 0] - t * per_owner, 0, per_owner - 1)
        chosen = (pick * held[pl.ds(row, 1), :]).astype(BF16)
        full = jnp.dot(chosen, place, preferred_element_type=F32)
        wide_ref[t] = jnp.where(same, full, 0.0).astype(BF16)


NT_DIMS = (((1,), (1,)), ((), ()))


def half_rows(tiles, mix, mixed, halves):
    ntiles = halves.shape[0]
    rows, cols = iota2((AREA, AREA), 0), iota2((AREA, AREA), 1)
    swap = ((rows % BLK == cols // BLK) & (rows // BLK == cols % BLK)).astype(BF16)
    for k in range(ntiles):
        block = jnp.concatenate([ref[:, k * AREA:(k + 1) * AREA] for ref in tiles], axis=0)
        turned = lax.dot_general(swap, block, NT_DIMS, preferred_element_type=F32).astype(BF16)
        for n in range(BLK):
            mixed[n, k * BLK:(k + 1) * BLK, :] = turned[n * BLK:(n + 1) * BLK, :]
    for n in range(BLK):
        half = jnp.dot(mix, mixed[n], preferred_element_type=F32).astype(BF16)
        for t in range(ntiles):
            halves[t, n * BLK:(n + 1) * BLK, :] = half[t * BLK:(t + 1) * BLK, :]


def k_own_body(tile_ref, mix_ref, wide_ref, out_ref, mixed, halves):
    half_rows((tile_ref,), mix_ref[...], mixed, halves)
    for t in range(wide_ref.shape[0]):
        out_ref[:, t * AREA:(t + 1) * AREA] = lax.dot_general(
            halves[t], wide_ref[t], (((0,), (1,)), ((), ())), preferred_element_type=F32
        ).astype(BF16)


def k_moved_body(inner_ref, outer_ref, mix_ref, wide_ref, out_ref, mixed, halves):
    half_rows((inner_ref, outer_ref), mix_ref[...], mixed, halves)
    for t in range(wide_ref.shape[0]):
        out_ref[t * AREA:(t + 1) * AREA, :] = jnp.dot(
            wide_ref[t], halves[t], preferred_element_type=F32
        ).astype(BF16)


def packed(top, bottom):
    half = top.shape[0] // 2
    return jnp.concatenate([top[:half], top[half:], bottom[:half], bottom[half:]], axis=1)


def arranged(top, bottom):
    cut = far_cut(top.shape[1])
    return jnp.concatenate([packed(top[:, :cut], bottom[:, :cut]), packed(top[:, cut:], bottom[:, cut:])], axis=1)


def far_cut(aux):
    return aux // 256 * 256 or aux // 2


def dot_rows(left, right):
    return lax.dot_general(left, right, NT_DIMS, preferred_element_type=F32)


def near_body(o_ref, p_ref, k_ref, out_ref):
    right = k_ref[...]
    out_ref[...] = arranged(dot_rows(o_ref[...], right), dot_rows(p_ref[...], right))


def place_of():
    plane, red = lax.axis_index("pair") // CORES, lax.axis_index("red")
    near = plane < 2
    return jnp.where(near, plane, 3 - plane), jnp.where(near, red, 3 - red)


def early_body(o_ref, p_ref, e_ref, f_ref, g_ref, kt_ref, near_ref, own_ref, s1, s2, s3, held_ref, terms):
    aux = o_ref.shape[0]
    right = kt_ref[...]
    top = jnp.dot(o_ref[...], right, preferred_element_type=F32)
    bottom = jnp.dot(p_ref[...], right, preferred_element_type=F32)
    terms[0] = near_ref[...]
    terms[1] = arranged(top[:, aux:], bottom[:, aux:])
    terms[2] = arranged(top[:, :aux], bottom[:, :aux])
    inner = kt_ref[:, :aux]
    lower = jnp.concatenate([f_ref[...], g_ref[...]], axis=0)
    terms[3] = arranged(
        jnp.dot(e_ref[...], inner, preferred_element_type=F32), jnp.dot(lower, inner, preferred_element_type=F32)
    )
    plane, place = place_of()
    hub = plane == 1

    def term_for(column):
        return jnp.where(hub, jnp.where(column < 2, 1 - column, column), jnp.minimum(column, 1))

    mine = hub & (place < 3) | (plane == 0) & (place < 2)
    own_ref[...] = jnp.where(mine, terms[term_for(place)], 0.0)
    for d, out in zip((1, 2, 3), (s1, s2, s3)):
        out[...] = terms[term_for(place ^ d)].astype(BF16)
    held_ref[...] = terms[3].astype(BF16)


LATE = ((2, 0, None, 1), (0, 2, None, None), (None, None, 0, 2), (None, None, 2, None))
FILLED = (0,)
LATE_TO = {0: (1, 3), 1: (0, 2), 2: (0, 3)}


def by_place(place, values):
    chosen = jnp.int32(values[3] or 0)
    for at in (2, 1, 0):
        chosen = jnp.where(place == at, values[at] or 0, chosen)
    return chosen


def late_body(k_ref, o_ref, p_ref, e_ref, f_ref, g_ref, held_ref, own_ref, s1, s2, s3, s4, terms):
    right = k_ref[...]
    plane, place = place_of()
    lower = jnp.concatenate([f_ref[...], g_ref[...]], axis=0)
    near = packed(dot_rows(o_ref[...], right), dot_rows(p_ref[...], right))
    own_ref[...] = jnp.where((plane == 1) & (place == 3), near, 0.0)
    terms[0] = near.astype(BF16)
    terms[1] = held_ref[...]
    terms[2] = packed(dot_rows(e_ref[...], right), dot_rows(lower, right)).astype(BF16)
    for sent, out in zip(LATE, (s1, s2, s3, s4)):
        out[...] = terms[by_place(place, sent)]


def last_body(k_ref, o_ref, p_ref, e_ref, f_ref, g_ref, held_ref, *refs):
    first, (own_ref, s1, s2, s3, s4, terms, own_part, t1, t2, t3, t4) = refs[:5], refs[5:]
    parts = (own_part, t1, t2, t3, t4)
    late_body(k_ref, o_ref, p_ref, e_ref, f_ref, g_ref, held_ref, *parts, terms)
    cut = first[0].shape[1]
    for out, before, part in zip((own_ref, s1, s2, s3, s4), first, parts):
        out[:, :cut] = before[...]
        out[:, cut:] = part[...]


def late_moves(sources):
    return [((1, g), LATE_TO[what]) for g, what in enumerate(sources) if what is not None]


def filled(moves):
    every = [(plane, g) for plane in range(2) for g in range(4)]
    sending, taking = [a for a, _ in moves], [b for _, b in moves]
    swaps = [at for at in every if at not in sending and at not in taking]
    rest = [at for at in every if at not in sending and at not in swaps]
    open_places = [at for at in every if at not in taking and at not in swaps]
    return moves + list(zip(rest, open_places)), swaps


def sum_body(*refs):
    values, sides = refs[:-2], refs[-2:]
    plane, place = place_of()

    def taken(index):
        found = jnp.bool_(False)
        for _, (a, g) in late_moves(LATE[index]):
            found = found | (plane == a) & (place == g)
        return found

    use = [None] * (len(values) - len(LATE)) + [taken(index) for index in range(len(LATE))]
    width = sides[0].shape[1]
    cut = far_cut(width // 2)
    for at, side in enumerate(sides):
        for start, size, to in ((at * 2 * cut, 2 * cut, 0), (4 * cut + at * (width - 2 * cut), width - 2 * cut, 2 * cut)):
            total = values[0][:, start:start + size]
            for value, wanted in zip(values[1:], use[1:]):
                piece = value[:, start:start + size].astype(F32)
                total = total + (piece if wanted is None else jnp.where(wanted, piece, 0.0))
            side[:, to:to + size] = total


def join_body(kept_ref, other_ref, out_ref):
    first = lax.axis_index("pair") % CORES == 0
    kept, other = kept_ref[...], other_ref[...]
    left, right = jnp.where(first, kept, other), jnp.where(first, other, kept)
    half, aux = left.shape[0], left.shape[1] // 2
    cut = far_cut(aux)
    for at in range(2):
        pieces = [
            piece
            for side in (left, right)
            for piece in (side[:, at * cut:(at + 1) * cut], side[:, 2 * cut + at * (aux - cut):2 * cut + (at + 1) * (aux - cut)])
        ]
        out_ref[at * half:(at + 1) * half, :] = jnp.concatenate(pieces, axis=1)


def call(body, outs, ins, scratch=(), smem=0, name=None):
    return pl.pallas_call(
        body,
        out_shape=outs,
        in_specs=[pl.BlockSpec(memory_space=pltpu.SMEM)] * smem
        + [pl.BlockSpec(memory_space=pltpu.VMEM)] * (len(ins) - smem),
        out_specs=jax.tree.map(lambda _: pl.BlockSpec(memory_space=pltpu.VMEM), outs),
        scratch_shapes=list(scratch),
        compiler_params=pltpu.CompilerParams(vmem_limit_bytes=VMEM_BYTES),
        cost_estimate=pl.CostEstimate(
            flops=1, transcendentals=0, bytes_accessed=1
        ),
        name=name,
    )(*ins)


def shaped(*shape, dtype=BF16):
    return jax.ShapeDtypeStruct(shape, dtype)


def hub_plan(three_center, occ_src, occ_block, occ_blocks, virt_block, virt_blocks):
    aux, ntiles, area = three_center.shape
    depth = ntiles * area

    def along_z(moves):
        return [(CORES * a + c, CORES * b + c) for a, b in moves for c in range(CORES)]

    core_swap = [(i, i ^ 1) for i in range(8)]
    both = ("pair", "red")

    def everywhere(moves, swaps=()):
        def pairs(found, flip):
            full = list(found) + [((3 - a, 3 - g), (3 - b, 3 - h)) for (a, g), (b, h) in found]
            return [
                ((CORES * a + c) * 4 + g, (CORES * b + (c ^ flip)) * 4 + h)
                for (a, g), (b, h) in full for c in range(CORES)
            ]

        return pairs(moves, 0) + pairs([(at, at) for at in swaps], 1)

    after = lax.optimization_barrier

    def scratch_for(count):
        return [pltpu.VMEM((BLK, ntiles * BLK, count), BF16), pltpu.VMEM((ntiles, area, count), BF16)]

    from_planes = [virt_blocks] + [
        lax.ppermute(virt_blocks, "pair", along_z([(a, a ^ k) for a in range(4)])) for k in (1, 2, 3)
    ]
    tiles = three_center.reshape(aux, depth)
    *from_planes, tiles = after((*from_planes, tiles))
    inner = lax.ppermute(tiles, "pair", along_z([(1, 2), (2, 1)]) + [(0, 1), (1, 0), (6, 7), (7, 6)])
    mine = jnp.concatenate(from_planes)
    theirs = lax.ppermute(mine, "pair", core_swap)
    partner = lax.ppermute(tiles, "pair", core_swap)
    theirs, tiles = after((theirs, tiles))
    outer = lax.ppermute(tiles, "pair", along_z([(0, 1), (1, 0), (2, 3), (3, 2)]))
    mix, wide = call(
        prep_body,
        [shaped(ntiles * BLK, ntiles * BLK), shaped(ntiles, area, area)],
        [occ_src, occ_block, virt_block, occ_blocks, mine, theirs],
        [
            pltpu.VMEM((occ_blocks.shape[0], BLK, ntiles * BLK), F32),
            pltpu.VMEM((CORES * mine.shape[0] * mine.shape[1], area), F32),
        ],
        smem=3, name="prep",
    )
    partner, wide, tiles = after((partner, wide, tiles))
    k_own = call(k_own_body, shaped(aux, depth), [tiles, mix, wide], scratch_for(aux), name="k_own")
    cut = far_cut(aux)
    far = [lax.ppermute(part, "pair", along_z([(0, 2), (3, 1)])) for part in (k_own[:cut], k_own[cut:])]
    term = (aux // 2, 4 * aux)
    near = call(near_body, shaped(*term, dtype=F32), [tiles, partner, k_own], name="near")
    outer, inner, near = after((outer, inner, near))

    outer_partner = [lax.ppermute(outer[at:at + aux // 2], "pair", core_swap) for at in (0, aux // 2)]
    k_moved = call(
        k_moved_body, shaped(depth, 2 * aux), [inner, outer, mix, wide], scratch_for(2 * aux), name="k_moved"
    )
    own_early, *sent, held = call(
        early_body,
        [shaped(*term, dtype=F32)] + [shaped(*term)] * 4,
        [tiles, partner, outer, *outer_partner, k_moved, near],
        [pltpu.VMEM((4, *term), F32)],
        name="early",
    )
    arrived = []
    for d, value in reversed(list(zip((1, 2, 3), sent))):
        moves = [((1, g), (1, g ^ d)) for g in range(4) if g ^ d != 3]
        moves += [((0, g), (0, g ^ d)) for g in range(4) if g ^ d < 2]
        moves += [((1, 3 ^ d), (0, 2))]
        arrived.append(lax.ppermute(value, both, everywhere(moves)))

    far[0], held = after((far[0], held))
    part = (aux // 2, 4 * cut)
    first_part = call(
        late_body,
        [shaped(*part, dtype=F32)] + [shaped(*part)] * 4,
        [far[0], tiles, partner, outer, *outer_partner, held[:, :4 * cut]],
        [pltpu.VMEM((3, *part), BF16)],
        name="late",
    )
    far[1], *first_part = after((far[1], *first_part))
    rest = (aux // 2, 4 * (aux - cut))
    own_late, *late_sent = call(
        last_body,
        [shaped(*term, dtype=F32)] + [shaped(*term)] * 4,
        [far[1], tiles, partner, outer, *outer_partner, held[:, 4 * cut:], *first_part],
        [pltpu.VMEM((3, *rest), BF16), pltpu.VMEM(rest, F32)] + [pltpu.VMEM(rest, BF16)] * 4,
        name="last",
    )
    for index, (sources, value) in enumerate(zip(LATE, late_sent)):
        moves = late_moves(sources)
        arrived.append(lax.ppermute(value, both, everywhere(*(filled(moves) if index in FILLED else (moves,)))))
    mine, yours = call(
        sum_body, [shaped(aux // 2, 2 * aux, dtype=F32)] * 2, [own_early, own_late, *arrived], name="sum"
    )
    other = lax.ppermute(yours, "pair", core_swap)
    return call(join_body, shaped(aux, 2 * aux, dtype=F32), [mine, other], name="join")


def solution(mesh):
    placed = (
        P("pair", "red", None),
        P("red", None),
        P("red", None),
        P("red", None),
        P("red", None, None),
        P("red", "pair", None),
    )
    line = mesh.shape["pair"] == 4 * CORES and mesh.shape["red"] == 4

    def shards(three_center, occ_src, occ_block, occ_blocks, virt_block, virt_blocks):
        owned = virt_block.shape[2] == 1 and virt_block.shape[1] == mesh.shape["pair"]
        plan = hub_plan if line and owned and three_center.shape[0] % 32 == 0 else gather_plan
        return plan(three_center, occ_src, occ_block, occ_blocks, virt_block, virt_blocks)

    return jax.shard_map(shards, mesh=mesh, in_specs=placed, out_specs=P("pair", "red"), check_vma=False)
```

```python
import functools

import jax
import jax.numpy as jnp
from jax import lax
from jax.experimental import pallas as pl
from jax.experimental.pallas import tpu as pltpu
from jax.sharding import PartitionSpec as P

BLK = 16
AREA = BLK * BLK
VMEM_BYTES = 24 * 1024 * 1024
CORES = 2
BF16 = jnp.bfloat16
F32 = jnp.float32


def mixing_of(occ_src, occ_block, occ_blocks, ntiles):
    nblocks = occ_blocks.shape[0]
    block_hot = (occ_block[:, :, None] == jnp.arange(nblocks, dtype=jnp.int32)).astype(BF16)
    picked = jnp.einsum("tsb,bk->tsk", block_hot, occ_blocks, preferred_element_type=F32).astype(BF16)
    source_hot = (occ_src[:, :, None] == jnp.arange(ntiles, dtype=jnp.int32)).astype(BF16)
    mixing = jnp.einsum("tsk,tsa->tka", source_hot, picked, preferred_element_type=F32).astype(BF16)
    return mixing.reshape(ntiles, ntiles, BLK, BLK)


def gather_plan(three_center, occ_src, occ_block, occ_blocks, virt_block, virt_blocks):
    aux_rows, ntiles, area = three_center.shape
    tpd = virt_block.shape[2]
    mixing = mixing_of(occ_src, occ_block, occ_blocks, ntiles)
    blocks = three_center.reshape(aux_rows, ntiles, BLK, BLK)
    half = jnp.einsum("tkml,pkln->ptmn", mixing, blocks, preferred_element_type=F32).astype(BF16)
    all_blocks = lax.all_gather(virt_blocks[0], "pair", axis=0, tiled=True)
    listed = virt_block[0].reshape(ntiles // tpd, tpd, tpd)
    block_hot = (listed[..., None] == jnp.arange(all_blocks.shape[0], dtype=jnp.int32)).astype(BF16)
    picked = jnp.einsum("oijb,bk->oijk", block_hot, all_blocks, preferred_element_type=F32).astype(BF16)
    picked = picked.reshape(ntiles // tpd, tpd, tpd, BLK, BLK)
    grouped = half.reshape(aux_rows, ntiles // tpd, tpd, BLK, BLK)
    kernel = jnp.einsum("pojml,oijln->poimn", grouped, picked, preferred_element_type=F32)
    kernel = kernel.reshape(aux_rows, ntiles, area).astype(BF16)
    piece = lax.all_gather(kernel, "pair", axis=0, tiled=True)
    partial_value = lax.dot_general(
        three_center.reshape(aux_rows, ntiles * area),
        piece.reshape(piece.shape[0], ntiles * area),
        (((1,), (1,)), ((), ())),
        preferred_element_type=F32,
    )
    return lax.psum_scatter(partial_value, "red", scatter_dimension=1, tiled=True)


def iota2(shape, dim):
    return lax.broadcasted_iota(jnp.int32, shape, dim)


def prep_body(src_ref, block_ref, listed_ref, blocks_ref, mine_ref, theirs_ref, mix_ref, wide_ref, density, held):
    nblocks = blocks_ref.shape[0]
    ntiles, listed_sources = src_ref.shape
    width = ntiles * BLK
    repeat = (iota2((nblocks * BLK, nblocks), 0) // BLK == iota2((nblocks * BLK, nblocks), 1)).astype(BF16)
    rows = jnp.dot(repeat, blocks_ref[...], preferred_element_type=F32)
    rows = jnp.where(iota2(rows.shape, 0) % BLK == iota2(rows.shape, 1) // BLK, rows, 0.0).astype(BF16)
    spread = (iota2((AREA, width), 0) % BLK == iota2((AREA, width), 1) % BLK).astype(BF16)
    density[...] = jnp.dot(rows, spread, preferred_element_type=F32).reshape(nblocks, BLK, width)
    column = iota2((BLK, width), 1) // BLK
    for t in range(ntiles):
        line = jnp.zeros((BLK, width), F32)
        for s in range(listed_sources):
            line = line + jnp.where(column == src_ref[t, s], density[block_ref[t, s]], 0.0)
        mix_ref[t * BLK:(t + 1) * BLK, :] = line.astype(BF16)

    pair = lax.axis_index("pair")
    plane, core = pair // CORES, pair % CORES
    planes, per_owner, _ = mine_ref.shape
    for k in range(planes):
        held[k * per_owner:(k + 1) * per_owner, :] = mine_ref[k].astype(F32)
        held[(planes + k) * per_owner:(planes + k + 1) * per_owner, :] = theirs_ref[k].astype(F32)
    pick = (iota2((AREA, AREA), 0) % BLK == iota2((AREA, AREA), 1) % BLK).astype(F32)
    place = (iota2((AREA, AREA), 0) // BLK == iota2((AREA, AREA), 1) // BLK).astype(BF16)
    same = iota2((AREA, AREA), 0) // BLK == iota2((AREA, AREA), 1) % BLK
    for t in range(ntiles):
        k, flip = plane ^ (t // CORES), core ^ (t % CORES)
        row = (flip * planes + k) * per_owner + jnp.clip(listed_ref[0, t, 0] - t * per_owner, 0, per_owner - 1)
        chosen = (pick * held[pl.ds(row, 1), :]).astype(BF16)
        full = jnp.dot(chosen, place, preferred_element_type=F32)
        wide_ref[t] = jnp.where(same, full, 0.0).astype(BF16)


NT_DIMS = (((1,), (1,)), ((), ()))


def half_rows(tiles, mix, mixed, halves):
    ntiles = halves.shape[0]
    rows, cols = iota2((AREA, AREA), 0), iota2((AREA, AREA), 1)
    swap = ((rows % BLK == cols // BLK) & (rows // BLK == cols % BLK)).astype(BF16)
    for k in range(ntiles):
        block = jnp.concatenate([ref[:, k * AREA:(k + 1) * AREA] for ref in tiles], axis=0)
        turned = lax.dot_general(swap, block, NT_DIMS, preferred_element_type=F32).astype(BF16)
        for n in range(BLK):
            mixed[n, k * BLK:(k + 1) * BLK, :] = turned[n * BLK:(n + 1) * BLK, :]
    for n in range(BLK):
        half = jnp.dot(mix, mixed[n], preferred_element_type=F32).astype(BF16)
        for t in range(ntiles):
            halves[t, n * BLK:(n + 1) * BLK, :] = half[t * BLK:(t + 1) * BLK, :]


def k_own_body(tile_ref, mix_ref, wide_ref, out_ref, mixed, halves):
    half_rows((tile_ref,), mix_ref[...], mixed, halves)
    for t in range(wide_ref.shape[0]):
        out_ref[:, t * AREA:(t + 1) * AREA] = lax.dot_general(
            halves[t], wide_ref[t], (((0,), (1,)), ((), ())), preferred_element_type=F32
        ).astype(BF16)


def k_moved_body(inner_ref, outer_ref, mix_ref, wide_ref, out_ref, mixed, halves):
    half_rows((inner_ref, outer_ref), mix_ref[...], mixed, halves)
    for t in range(wide_ref.shape[0]):
        out_ref[t * AREA:(t + 1) * AREA, :] = jnp.dot(
            wide_ref[t], halves[t], preferred_element_type=F32
        ).astype(BF16)


def packed(top, bottom):
    half = top.shape[0] // 2
    return jnp.concatenate([top[:half], top[half:], bottom[:half], bottom[half:]], axis=1)


def arranged(top, bottom):
    cut = far_cut(top.shape[1])
    return jnp.concatenate([packed(top[:, :cut], bottom[:, :cut]), packed(top[:, cut:], bottom[:, cut:])], axis=1)


def far_cut(aux):
    return aux // 256 * 256 or aux // 2


def dot_rows(left, right):
    return lax.dot_general(left, right, NT_DIMS, preferred_element_type=F32)


def near_body(o_ref, p_ref, k_ref, out_ref):
    right = k_ref[...]
    out_ref[...] = arranged(dot_rows(o_ref[...], right), dot_rows(p_ref[...], right))


def place_of():
    plane, red = lax.axis_index("pair") // CORES, lax.axis_index("red")
    near = plane < 2
    return jnp.where(near, plane, 3 - plane), jnp.where(near, red, 3 - red)


def early_body(o_ref, p_ref, e_ref, f_ref, g_ref, kt_ref, near_ref, own_ref, s1, s2, s3, held_ref, terms):
    aux = o_ref.shape[0]
    right = kt_ref[...]
    top = jnp.dot(o_ref[...], right, preferred_element_type=F32)
    bottom = jnp.dot(p_ref[...], right, preferred_element_type=F32)
    terms[0] = near_ref[...]
    terms[1] = arranged(top[:, aux:], bottom[:, aux:])
    terms[2] = arranged(top[:, :aux], bottom[:, :aux])
    inner = kt_ref[:, :aux]
    lower = jnp.concatenate([f_ref[...], g_ref[...]], axis=0)
    terms[3] = arranged(
        jnp.dot(e_ref[...], inner, preferred_element_type=F32), jnp.dot(lower, inner, preferred_element_type=F32)
    )
    plane, place = place_of()
    hub = plane == 1

    def term_for(column):
        return jnp.where(hub, jnp.where(column < 2, 1 - column, column), jnp.minimum(column, 1))

    mine = hub & (place < 3) | (plane == 0) & (place < 2)
    own_ref[...] = jnp.where(mine, terms[term_for(place)], 0.0)
    for d, out in zip((1, 2, 3), (s1, s2, s3)):
        out[...] = terms[term_for(place ^ d)].astype(BF16)
    held_ref[...] = terms[3].astype(BF16)


LATE = ((0, 2, None, 1), (2, 0, None, None), (None, None, 0, 2), (None, None, 2, None))
FILLED = (0,)
LATE_TO = {0: (1, 3), 1: (0, 2), 2: (0, 3)}


def by_place(place, values):
    chosen = jnp.int32(values[3] or 0)
    for at in (2, 1, 0):
        chosen = jnp.where(place == at, values[at] or 0, chosen)
    return chosen


def late_body(k_ref, o_ref, p_ref, e_ref, f_ref, g_ref, held_ref, own_ref, s1, s2, s3, s4, terms):
    right = k_ref[...]
    plane, place = place_of()
    lower = jnp.concatenate([f_ref[...], g_ref[...]], axis=0)
    near = packed(dot_rows(o_ref[...], right), dot_rows(p_ref[...], right))
    own_ref[...] = jnp.where((plane == 1) & (place == 3), near, 0.0)
    terms[0] = near.astype(BF16)
    terms[1] = held_ref[...]
    terms[2] = packed(dot_rows(e_ref[...], right), dot_rows(lower, right)).astype(BF16)
    for sent, out in zip(LATE, (s1, s2, s3, s4)):
        out[...] = terms[by_place(place, sent)]


def last_body(k_ref, o_ref, p_ref, e_ref, f_ref, g_ref, held_ref, *refs):
    first, (own_ref, s1, s2, s3, s4, terms, own_part, t1, t2, t3, t4) = refs[:5], refs[5:]
    parts = (own_part, t1, t2, t3, t4)
    late_body(k_ref, o_ref, p_ref, e_ref, f_ref, g_ref, held_ref, *parts, terms)
    cut = first[0].shape[1]
    for out, before, part in zip((own_ref, s1, s2, s3, s4), first, parts):
        out[:, :cut] = before[...]
        out[:, cut:] = part[...]


def late_moves(sources):
    return [((1, g), LATE_TO[what]) for g, what in enumerate(sources) if what is not None]


def filled(moves):
    every = [(plane, g) for plane in range(2) for g in range(4)]
    sending, taking = [a for a, _ in moves], [b for _, b in moves]
    swaps = [at for at in every if at not in sending and at not in taking]
    rest = [at for at in every if at not in sending and at not in swaps]
    open_places = [at for at in every if at not in taking and at not in swaps]
    return moves + list(zip(rest, open_places)), swaps


def sum_body(*refs):
    values, sides = refs[:-2], refs[-2:]
    plane, place = place_of()

    def taken(index):
        found = jnp.bool_(False)
        for _, (a, g) in late_moves(LATE[index]):
            found = found | (plane == a) & (place == g)
        return found

    use = [None] * (len(values) - len(LATE)) + [taken(index) for index in range(len(LATE))]
    width = sides[0].shape[1]
    cut = far_cut(width // 2)
    for at, side in enumerate(sides):
        for start, size, to in ((at * 2 * cut, 2 * cut, 0), (4 * cut + at * (width - 2 * cut), width - 2 * cut, 2 * cut)):
            total = values[0][:, start:start + size]
            for value, wanted in zip(values[1:], use[1:]):
                piece = value[:, start:start + size].astype(F32)
                total = total + (piece if wanted is None else jnp.where(wanted, piece, 0.0))
            side[:, to:to + size] = total


def join_body(kept_ref, other_ref, out_ref):
    first = lax.axis_index("pair") % CORES == 0
    kept, other = kept_ref[...], other_ref[...]
    left, right = jnp.where(first, kept, other), jnp.where(first, other, kept)
    half, aux = left.shape[0], left.shape[1] // 2
    cut = far_cut(aux)
    for at in range(2):
        pieces = [
            piece
            for side in (left, right)
            for piece in (side[:, at * cut:(at + 1) * cut], side[:, 2 * cut + at * (aux - cut):2 * cut + (at + 1) * (aux - cut)])
        ]
        out_ref[at * half:(at + 1) * half, :] = jnp.concatenate(pieces, axis=1)


def call(body, outs, ins, scratch=(), smem=0, name=None):
    return pl.pallas_call(
        body,
        out_shape=outs,
        in_specs=[pl.BlockSpec(memory_space=pltpu.SMEM)] * smem
        + [pl.BlockSpec(memory_space=pltpu.VMEM)] * (len(ins) - smem),
        out_specs=jax.tree.map(lambda _: pl.BlockSpec(memory_space=pltpu.VMEM), outs),
        scratch_shapes=list(scratch),
        compiler_params=pltpu.CompilerParams(vmem_limit_bytes=VMEM_BYTES),
        cost_estimate=pl.CostEstimate(
            flops=1, transcendentals=0, bytes_accessed=1
        ),
        name=name,
    )(*ins)


def shaped(*shape, dtype=BF16):
    return jax.ShapeDtypeStruct(shape, dtype)


def hub_plan(three_center, occ_src, occ_block, occ_blocks, virt_block, virt_blocks):
    aux, ntiles, area = three_center.shape
    depth = ntiles * area

    def along_z(moves):
        return [(CORES * a + c, CORES * b + c) for a, b in moves for c in range(CORES)]

    core_swap = [(i, i ^ 1) for i in range(8)]
    both = ("pair", "red")

    def everywhere(moves, swaps=()):
        def pairs(found, flip):
            full = list(found) + [((3 - a, 3 - g), (3 - b, 3 - h)) for (a, g), (b, h) in found]
            return [
                ((CORES * a + c) * 4 + g, (CORES * b + (c ^ flip)) * 4 + h)
                for (a, g), (b, h) in full for c in range(CORES)
            ]

        return pairs(moves, 0) + pairs([(at, at) for at in swaps], 1)

    after = lax.optimization_barrier

    def scratch_for(count):
        return [pltpu.VMEM((BLK, ntiles * BLK, count), BF16), pltpu.VMEM((ntiles, area, count), BF16)]

    from_planes = [virt_blocks] + [
        lax.ppermute(virt_blocks, "pair", along_z([(a, a ^ k) for a in range(4)])) for k in (1, 2, 3)
    ]
    tiles = three_center.reshape(aux, depth)
    *from_planes, tiles = after((*from_planes, tiles))
    inner = lax.ppermute(tiles, "pair", along_z([(1, 2), (2, 1)]) + [(0, 1), (1, 0), (6, 7), (7, 6)])
    mine = jnp.concatenate(from_planes)
    theirs = lax.ppermute(mine, "pair", core_swap)
    partner = lax.ppermute(tiles, "pair", core_swap)
    theirs, tiles = after((theirs, tiles))
    outer = lax.ppermute(tiles, "pair", along_z([(0, 1), (1, 0), (2, 3), (3, 2)]))
    mix, wide = call(
        prep_body,
        [shaped(ntiles * BLK, ntiles * BLK), shaped(ntiles, area, area)],
        [occ_src, occ_block, virt_block, occ_blocks, mine, theirs],
        [
            pltpu.VMEM((occ_blocks.shape[0], BLK, ntiles * BLK), F32),
            pltpu.VMEM((CORES * mine.shape[0] * mine.shape[1], area), F32),
        ],
        smem=3, name="prep",
    )
    partner, wide, tiles = after((partner, wide, tiles))
    k_own = call(k_own_body, shaped(aux, depth), [tiles, mix, wide], scratch_for(aux), name="k_own")
    cut = far_cut(aux)
    far = [lax.ppermute(part, "pair", along_z([(0, 2), (3, 1)])) for part in (k_own[:cut], k_own[cut:])]
    term = (aux // 2, 4 * aux)
    near = call(near_body, shaped(*term, dtype=F32), [tiles, partner, k_own], name="near")
    outer, inner, near = after((outer, inner, near))

    outer_partner = [lax.ppermute(outer[at:at + aux // 2], "pair", core_swap) for at in (0, aux // 2)]
    k_moved = call(
        k_moved_body, shaped(depth, 2 * aux), [inner, outer, mix, wide], scratch_for(2 * aux), name="k_moved"
    )
    own_early, *sent, held = call(
        early_body,
        [shaped(*term, dtype=F32)] + [shaped(*term)] * 4,
        [tiles, partner, outer, *outer_partner, k_moved, near],
        [pltpu.VMEM((4, *term), F32)],
        name="early",
    )
    arrived = []
    for d, value in reversed(list(zip((1, 2, 3), sent))):
        moves = [((1, g), (1, g ^ d)) for g in range(4) if g ^ d != 3]
        moves += [((0, g), (0, g ^ d)) for g in range(4) if g ^ d < 2]
        moves += [((1, 3 ^ d), (0, 2))]
        arrived.append(lax.ppermute(value, both, everywhere(moves)))

    far[0], held = after((far[0], held))
    part = (aux // 2, 4 * cut)
    first_part = call(
        late_body,
        [shaped(*part, dtype=F32)] + [shaped(*part)] * 4,
        [far[0], tiles, partner, outer, *outer_partner, held[:, :4 * cut]],
        [pltpu.VMEM((3, *part), BF16)],
        name="late",
    )
    far[1], *first_part = after((far[1], *first_part))
    rest = (aux // 2, 4 * (aux - cut))
    own_late, *late_sent = call(
        last_body,
        [shaped(*term, dtype=F32)] + [shaped(*term)] * 4,
        [far[1], tiles, partner, outer, *outer_partner, held[:, 4 * cut:], *first_part],
        [pltpu.VMEM((3, *rest), BF16), pltpu.VMEM(rest, F32)] + [pltpu.VMEM(rest, BF16)] * 4,
        name="last",
    )
    for index, (sources, value) in enumerate(zip(LATE, late_sent)):
        moves = late_moves(sources)
        arrived.append(lax.ppermute(value, both, everywhere(*(filled(moves) if index in FILLED else (moves,)))))
    mine, yours = call(
        sum_body, [shaped(aux // 2, 2 * aux, dtype=F32)] * 2, [own_early, own_late, *arrived], name="sum"
    )
    other = lax.ppermute(yours, "pair", core_swap)
    return call(join_body, shaped(aux, 2 * aux, dtype=F32), [mine, other], name="join")


def solution(mesh):
    placed = (
        P("pair", "red", None),
        P("red", None),
        P("red", None),
        P("red", None),
        P("red", None, None),
        P("red", "pair", None),
    )
    line = mesh.shape["pair"] == 4 * CORES and mesh.shape["red"] == 4

    def shards(three_center, occ_src, occ_block, occ_blocks, virt_block, virt_blocks):
        owned = virt_block.shape[2] == 1 and virt_block.shape[1] == mesh.shape["pair"]
        plan = hub_plan if line and owned and three_center.shape[0] % 32 == 0 else gather_plan
        return plan(three_center, occ_src, occ_block, occ_blocks, virt_block, virt_blocks)

    return jax.shard_map(shards, mesh=mesh, in_specs=placed, out_specs=P("pair", "red"), check_vma=False)
```
